32 devices in a mesh: section: 2 (over x), wide: 16 (over z, y, core).
Axes of the slice: x: 2, y: 2, z: 4, core: 2. Of those that a mesh axis runs over, the one named last changes fastest.
Arguments:
- features: float32 [2, 5120, 512], P(None, 'wide'), may hold values from -6 to 6
- sigma_embed: bfloat16 [2, 512], replicated, may hold values from -6 to 6
- cotangent: float32 [2, 5120, 512], P(None, 'wide'), may hold values from -6 to 6
- neighbours: int32 [5120, 16], P('wide'), may hold values from 0 to 5119, as said below
- valid_slots: int32 [5120, 16], P('wide'), may hold values from 0 to 1, as said below
- ada_weight: bfloat16 [2, 512, 2048], P('section'), may hold values from -0.0625 to 0.0625
- ada_bias: float32 [2, 2048], P('section'), may hold values from -4 to 4
- qkv_weight: bfloat16 [2, 512, 1536], P('section'), may hold values from -0.25 to 0.25
- out_weight: bfloat16 [2, 512, 512], P('section'), may hold values from -1 to 1
- up_weight: bfloat16 [2, 512, 2048], P('section'), may hold values from -0.25 to 0.25
- up_bias: float32 [2, 2048], P('section'), may hold values from -6 to 6
- down_weight: bfloat16 [2, 2048, 512], P('section'), may hold values from -0.125 to 0.125
- down_bias: float32 [2, 512], P('section'), may hold values from -4 to 4
Outputs:
- boundary: float32 [2, 2, 5120, 512], P('section', None, 'wide')
- grad_ada_weight: float32 [2, 512, 2048], P('section')
- grad_ada_bias: float32 [2, 2048], P('section')
- grad_qkv_weight: float32 [2, 512, 1536], P('section')
- grad_out_weight: float32 [2, 512, 512], P('section')
- grad_up_weight: float32 [2, 512, 2048], P('section')
- grad_up_bias: float32 [2, 2048], P('section')
- grad_down_weight: float32 [2, 2048, 512], P('section')
- grad_down_bias: float32 [2, 512], P('section')
The draws below stay inside these ranges and needn't reach their ends.
Inputs may be any that keep to these rules, and one draw needn't show every extreme that they name: `neighbours`: node numbers of one micro-batch's mesh; column 0 is the node itself; every entry lies within 320 places of its node, counted cyclically over 5120, and that distance is met in both directions. `valid_slots`: column 0 is always 1.
All inputs are finite; a program needn't handle non-finite values.
Results may differ from the reference program's by a relative error of at most 0.015.
Values may be sent and summed in bfloat16 or wider, within the bound.
A program may use at most 192 MiB of HBM per device.

```python
import math
import jax
import jax.numpy as jnp
from jax import lax

D = 512
FF = 2048
HEADS = 4
HEAD_DIM = 128
COND = 512
NEIGHBOURS = 16
NODE_DEV = 320
MICRO = 2
LAYERS = 2
NODES = 5120


def draw_neighbours(key, part):
    key = jax.random.fold_in(key, 11)
    offsets = jax.random.randint(key, (NODES, NEIGHBOURS), -NODE_DEV, NODE_DEV + 1)
    node_ids = jnp.arange(NODES, dtype=jnp.int32)[:, None]
    column_ids = jnp.arange(NEIGHBOURS, dtype=jnp.int32)[None, :]
    offsets = jnp.where(column_ids == 0, 0, offsets)
    forced_offset = jnp.where(node_ids % 7 == 0, NODE_DEV, jnp.where(node_ids % 7 == 1, -NODE_DEV, offsets[:, NEIGHBOURS - 1:]))
    offsets = jnp.where(column_ids == NEIGHBOURS - 1, forced_offset, offsets)
    return jnp.remainder(node_ids + offsets, NODES).astype(jnp.int32)


def draw_valid_slots(key, part):
    key = jax.random.fold_in(key, 23)
    coins = jax.random.randint(key, (NODES, NEIGHBOURS), 0, 4)
    column_ids = jnp.arange(NEIGHBOURS, dtype=jnp.int32)[None, :]
    return jnp.where((column_ids == 0) | (coins > 0), 1, 0).astype(jnp.int32)


def steps_of(own_key, extent, cuts, smallest, high):
    factor_of = 1.0
    for dim, blocks in cuts:
        heights = jax.random.uniform(jax.random.fold_in(jax.random.fold_in(own_key, 6), dim), (blocks,), jnp.float32, smallest / len(cuts), high / len(cuts))
        factor_of = factor_of * jnp.repeat(jnp.exp(heights), extent[dim] // blocks).reshape((-1,) + (1,) * (len(extent) - 1 - dim))
    return factor_of


def centred(stream_key, shape, scale, most, shards=(), kind=jnp.bfloat16):
    level = steps_of(stream_key, shape, shards, -0.22, 0.18) if shards else 1.0
    values = jax.random.normal(stream_key, shape, jnp.float32) * scale * level
    return jnp.minimum(jnp.maximum(values, -most), most).astype(kind)


def setup_inputs(seed: int = 0) -> dict:
    key_list = jax.random.split(jax.random.key(seed), 14)
    features = centred(key_list[0], (MICRO, NODES, D), 1.0, 6.0, ((1, 16),), jnp.float32)
    sigma_embed = centred(key_list[1], (MICRO, COND), 1.0, 6.0)
    cotangent = centred(key_list[2], (MICRO, NODES, D), 1.0, 6.0, ((1, 16),), jnp.float32)
    neighbours = draw_neighbours(jax.random.fold_in(key_list[13], 71), 0)
    valid_slots = draw_valid_slots(jax.random.fold_in(key_list[13], 71), 0)
    ada_weight = centred(key_list[5], (LAYERS, COND, 4 * D), (COND * 16) ** -0.5, 0.0625, ((0, 2),))
    ada_bias = centred(key_list[6], (LAYERS, 4 * D), 0.3, 4.0, ((0, 2),), jnp.float32)
    qkv_weight = centred(key_list[7], (LAYERS, D, 3 * D), D ** -0.5, 0.25, ((0, 2),))
    out_weight = centred(key_list[8], (LAYERS, D, D), (D // 16) ** -0.5, 1.0, ((0, 2),))
    up_weight = centred(key_list[9], (LAYERS, D, FF), D ** -0.5, 0.25, ((0, 2),))
    up_bias = centred(key_list[10], (LAYERS, FF), 0.5, 6.0, ((0, 2),), jnp.float32)
    down_weight = centred(key_list[11], (LAYERS, FF, D), FF ** -0.5, 0.125, ((0, 2),))
    down_bias = centred(key_list[12], (LAYERS, D), 0.3, 4.0, ((0, 2),), jnp.float32)
    return dict(features=features, sigma_embed=sigma_embed, cotangent=cotangent, neighbours=neighbours, valid_slots=valid_slots, ada_weight=ada_weight, ada_bias=ada_bias, qkv_weight=qkv_weight, out_weight=out_weight, up_weight=up_weight, up_bias=up_bias, down_weight=down_weight, down_bias=down_bias)


@jax.custom_vjp
def low(v):
    return lax.optimization_barrier(v.astype(jnp.bfloat16)).astype(jnp.float32)

@jax.custom_vjp
def low_back(v):
    return v

def low_keep(v):
    return (low(v), None)

def low_pass(kept, grad):
    return (grad,)

def back_keep(v):
    return (v, None)

def back_low(kept, grad):
    return (low(grad),)
low.defvjp(low_keep, low_pass)
low_back.defvjp(back_keep, back_low)
norm_epsilon = 1e-05
masked_score = -1e+30

def matmul(left, right):
    return jnp.dot(left, right, precision=lax.Precision.HIGHEST)

def normalize(values):
    center = values - lax.optimization_barrier(jnp.mean(values, axis=-1, keepdims=True))
    spread = lax.optimization_barrier(jnp.mean(center * center, axis=-1, keepdims=True))
    return center * lax.rsqrt(spread + norm_epsilon)

def attend_block(queries, key_value, node_index, slot_mask):
    row_count = queries.shape[0]
    near_rows = key_value[node_index]
    key_heads = near_rows[:, :, :D].reshape(row_count, NEIGHBOURS, HEADS, HEAD_DIM)
    value_heads = near_rows[:, :, D:].reshape(row_count, NEIGHBOURS, HEADS, HEAD_DIM)
    query_heads = queries.reshape(row_count, HEADS, HEAD_DIM)
    scores = jnp.einsum('nhe,nkhe->nkh', query_heads, key_heads, precision=lax.Precision.HIGHEST) * HEAD_DIM ** (-0.5)
    scores = jnp.where(slot_mask[:, :, None] > 0, scores, masked_score)
    row_top = lax.optimization_barrier(jnp.max(scores, axis=1, keepdims=True))
    raised = jnp.exp(scores - row_top)
    soft_weights = raised / lax.optimization_barrier(jnp.sum(raised, axis=1, keepdims=True))
    attended = jnp.einsum('nkh,nkhe->nhe', soft_weights, value_heads, precision=lax.Precision.HIGHEST)
    return attended.reshape(row_count, D)

def layer(params, layer_in, embed_row, neighbours, valid_slots):
    ada_weight, ada_bias, qkv_weight, out_weight, up_weight, up_bias, down_weight, down_bias = params
    modulation = matmul(embed_row[None, :], ada_weight)[0] + ada_bias
    shift_a = modulation[:D]
    scale_a = modulation[D:2 * D]
    shift_b = modulation[2 * D:3 * D]
    scale_b = modulation[3 * D:]
    normed_a = low(normalize(layer_in) * (1.0 + scale_a) + shift_a)
    mixed_qkv = low_back(low(matmul(normed_a, qkv_weight)))
    key_value = mixed_qkv[:, D:]
    block_rows = math.gcd(NODES, 512)
    blocks = NODES // block_rows

    def one_block(pieces):
        return attend_block(pieces[0], key_value, pieces[1], pieces[2])
    attended = lax.map(jax.checkpoint(one_block), (mixed_qkv[:, :D].reshape(blocks, block_rows, D), neighbours.reshape(blocks, block_rows, NEIGHBOURS), valid_slots.reshape(blocks, block_rows, NEIGHBOURS))).reshape(NODES, D)
    mixed = layer_in + low_back(matmul(low(attended), out_weight))
    normed_b = low(normalize(mixed) * (1.0 + scale_b) + shift_b)
    hidden = low_back(matmul(normed_b, up_weight) + up_bias)
    active = low(hidden * jax.nn.sigmoid(hidden))
    return mixed + low_back(matmul(active, down_weight)) + down_bias

def reference(features, sigma_embed, cotangent, neighbours, valid_slots, ada_weight, ada_bias, qkv_weight, out_weight, up_weight, up_bias, down_weight, down_bias):
    params = tuple((member.astype(jnp.float32) for member in (ada_weight, ada_bias, qkv_weight, out_weight, up_weight, up_bias, down_weight, down_bias)))
    embeds = sigma_embed.astype(jnp.float32)

    def forward(params, inputs):
        finals = []
        for micro_index in range(MICRO):
            first_out = layer(tuple((member[0] for member in params)), inputs[micro_index], embeds[micro_index], neighbours, valid_slots)
            passed = low_back(low(first_out))
            finals.append(layer(tuple((member[1] for member in params)), passed, embeds[micro_index], neighbours, valid_slots))
        return jnp.stack(finals)
    finals, pullback = jax.vjp(forward, params, features)
    weight_grads, grad_features = pullback(cotangent)
    boundary = jnp.stack([grad_features, finals])
    return (boundary, weight_grads[0], weight_grads[1], weight_grads[2], weight_grads[3], weight_grads[4], weight_grads[5], weight_grads[6], weight_grads[7])
```

```python
import jax
import jax.numpy as jnp
from jax import lax
from jax.sharding import PartitionSpec as P

D = 512
FF = 2048
HEADS = 4
HEAD_DIM = 128
NEIGHBOURS = 16
MICRO = 2


norm_epsilon = 1e-05
masked_score = -1e30


def with_halo(cells, sides, width):
    for axis, dim in sides:
        count = lax.axis_size(axis)
        head = lax.slice_in_dim(cells, 0, width, axis=dim)
        tail = lax.slice_in_dim(cells, cells.shape[dim] - width, cells.shape[dim], axis=dim)
        cells = jnp.concatenate(
            [
                lax.ppermute(tail, axis, [(i, (i + 1) % count) for i in range(count)]),
                cells,
                lax.ppermute(head, axis, [((i + 1) % count, i) for i in range(count)]),
            ],
            axis=dim,
        )
    return cells


def shifted(value, axis, steps):
    count = lax.axis_size(axis)
    first, last = (max(0, -steps), min(count, count - steps))
    return lax.ppermute(value, axis, [(source, source + steps) for source in range(first, last)])


def normalize(values):
    center = values - jnp.mean(values, axis=-1, keepdims=True)
    spread = jnp.mean(center * center, axis=-1, keepdims=True)
    return center * lax.rsqrt(spread + norm_epsilon)


def modulate(values, shift, scale):
    return normalize(values) * (1.0 + scale) + shift


def swish(values):
    return values * jax.nn.sigmoid(values)


def rows_product(left, right):
    return lax.dot_general(
        left, right, (((0,), (0,)), ((), ())), preferred_element_type=jnp.float32
    )


def cross_product(left, right):
    return lax.dot_general(
        left, right, (((1,), (1,)), ((), ())), preferred_element_type=jnp.float32
    )


def split_heads(packed):
    return packed.reshape(packed.shape[:-1] + (HEADS, HEAD_DIM))


def make_modulation(weights, embed_row):
    return (
        jnp.dot(embed_row[None, :], weights[0], preferred_element_type=jnp.float32)[0] + weights[1]
    )


def widen_rim(normed):
    return with_halo(normed, (("wide", 0),), normed.shape[0])


def pre_attention(layer_in, modulation, weights):
    normed_a = modulate(layer_in, modulation[:D], modulation[D : 2 * D]).astype(jnp.bfloat16)
    window = widen_rim(normed_a)
    queries = jnp.dot(normed_a, weights[2][:, :D], preferred_element_type=jnp.float32)
    key_value = jnp.dot(window, weights[2][:, D:], preferred_element_type=jnp.float32)
    return (window, queries.astype(jnp.bfloat16), key_value.astype(jnp.bfloat16))


def heads_of(packed, start=0):
    return [packed[:, start + h * HEAD_DIM : start + (h + 1) * HEAD_DIM] for h in range(HEADS)]


def attention_forward(queries, key_value, counts):
    attended, logs = [], []
    for query, key, value in zip(heads_of(queries), heads_of(key_value), heads_of(key_value, D)):
        scores = jnp.where(counts > 0, cross_product(query, key) * HEAD_DIM ** (-0.5), masked_score)
        row_top = jnp.max(scores, axis=1, keepdims=True)
        raised = jnp.exp(scores - row_top) * counts
        total_weight = jnp.sum(raised, axis=1, keepdims=True)
        part = jnp.dot(raised.astype(jnp.bfloat16), value, preferred_element_type=jnp.float32)
        attended.append(part / total_weight)
        logs.append(row_top + jnp.log(total_weight))
    return jnp.concatenate(attended, axis=1), jnp.concatenate(logs, axis=1)


def attention_backward(queries, key_value, counts, log_total, grad_attended):
    grad_q, grad_k, grad_v = [], [], []
    grad_low = grad_attended.astype(jnp.bfloat16)
    for h, (query, key, value, grad) in enumerate(
        zip(heads_of(queries), heads_of(key_value), heads_of(key_value, D), heads_of(grad_low))
    ):
        scores = cross_product(query, key) * HEAD_DIM ** (-0.5)
        soft = jnp.where(counts > 0, jnp.exp(scores - log_total[:, h : h + 1]) * counts, 0.0)
        grad_soft = cross_product(grad, value)
        inner = jnp.sum(soft * grad_soft, axis=1, keepdims=True)
        grad_scores = (soft * (grad_soft - inner) * HEAD_DIM ** (-0.5)).astype(jnp.bfloat16)
        grad_q.append(jnp.dot(grad_scores, key, preferred_element_type=jnp.float32))
        grad_k.append(rows_product(grad_scores, query))
        grad_v.append(rows_product(soft.astype(jnp.bfloat16), grad))
    return jnp.concatenate(grad_q, axis=1), jnp.concatenate(grad_k + grad_v, axis=1)


def layer_tail(layer_in, modulation, weights, rim_parts, counts):
    attended, log_total = attention_forward(rim_parts[1], rim_parts[2], counts)
    attended_low = attended.astype(jnp.bfloat16)
    mixed = layer_in + jnp.dot(attended_low, weights[3], preferred_element_type=jnp.float32)
    normed_b = modulate(mixed, modulation[2 * D : 3 * D], modulation[3 * D :]).astype(jnp.bfloat16)
    hidden = jnp.dot(normed_b, weights[4], preferred_element_type=jnp.float32) + weights[5]
    active = swish(hidden).astype(jnp.bfloat16)
    output = mixed + jnp.dot(active, weights[6], preferred_element_type=jnp.float32) + weights[7]
    return (output, (attended_low, log_total, mixed, normed_b, hidden, active))


def layer_backward(
    layer_in, modulation, weights, rim_parts, tail_parts, counts, grad_out
):
    window, queries, key_value = rim_parts
    attended_low, log_total, mixed, normed_b, hidden, active = tail_parts
    row_count = layer_in.shape[0]
    grad_low = grad_out.astype(jnp.bfloat16)
    grad_down = rows_product(active, grad_low)
    grad_down_bias = jnp.sum(grad_out, axis=0)
    grad_active = cross_product(grad_low, weights[6])
    swish_value, swish_back = jax.vjp(swish, hidden)
    grad_hidden = swish_back(grad_active)[0].astype(jnp.bfloat16)
    grad_up_bias = jnp.sum(grad_hidden.astype(jnp.float32), axis=0)
    grad_up = rows_product(normed_b, grad_hidden)
    grad_normed_b = cross_product(grad_hidden, weights[4])
    norm_value, norm_back = jax.vjp(modulate, mixed, modulation[2 * D : 3 * D], modulation[3 * D :])
    grad_mixed_part, grad_shift_b, grad_scale_b = norm_back(grad_normed_b)
    grad_mixed = grad_out + grad_mixed_part
    grad_mixed_low = grad_mixed.astype(jnp.bfloat16)
    grad_out_weight = rows_product(attended_low, grad_mixed_low)
    grad_attended = cross_product(grad_mixed_low, weights[3])
    grad_queries, grad_key_value = attention_backward(
        queries, key_value, counts, log_total, grad_attended
    )
    grad_queries = grad_queries.astype(jnp.bfloat16)
    grad_key_value = grad_key_value.astype(jnp.bfloat16)
    grad_qkv_weight = jnp.concatenate(
        [
            rows_product(window[row_count : 2 * row_count], grad_queries),
            rows_product(window, grad_key_value),
        ],
        axis=1,
    )
    grad_window = cross_product(grad_key_value, weights[2][:, D:])
    outer_rows = jnp.concatenate([grad_window[:row_count], grad_window[2 * row_count :]], axis=0)
    returned = with_halo(outer_rows.astype(jnp.bfloat16), (("wide", 0),), row_count)
    grad_normed_a = (
        cross_product(grad_queries, weights[2][:, :D])
        + grad_window[row_count : 2 * row_count]
        + returned[:row_count].astype(jnp.float32)
        + returned[3 * row_count :].astype(jnp.float32)
    )
    norm_value_a, norm_back_a = jax.vjp(modulate, layer_in, modulation[:D], modulation[D : 2 * D])
    grad_in_part, grad_shift_a, grad_scale_a = norm_back_a(grad_normed_a)
    grad_in = grad_mixed + grad_in_part
    grad_mod = jnp.concatenate([grad_shift_a, grad_scale_a, grad_shift_b, grad_scale_b])
    return (
        grad_in,
        grad_mod,
        (grad_qkv_weight, grad_out_weight, grad_up, grad_up_bias, grad_down, grad_down_bias),
    )


def recall(stored, position, empty):
    if 0 <= position < len(stored):
        return stored[position]
    return empty


def shards(
    features,
    sigma_embed,
    cotangent,
    neighbours,
    valid_slots,
    ada_weight,
    ada_bias,
    qkv_weight,
    out_weight,
    up_weight,
    up_bias,
    down_weight,
    down_bias,
):
    weights = (
        ada_weight[0],
        ada_bias[0],
        qkv_weight[0],
        out_weight[0],
        up_weight[0],
        up_bias[0],
        down_weight[0],
        down_bias[0],
    )
    row_count = features.shape[1]
    section_index = lax.axis_index("section")
    first_section = section_index == 0
    places = jnp.remainder(
        neighbours - (lax.axis_index("wide") - 1) * row_count, row_count * lax.axis_size("wide")
    )
    columns = lax.broadcasted_iota(jnp.int32, (row_count, 3 * row_count), 1)
    counts = jnp.zeros((row_count, 3 * row_count), jnp.float32)
    for slot in range(NEIGHBOURS):
        hit = (places[:, slot : slot + 1] == columns) & (valid_slots[:, slot : slot + 1] > 0)
        counts = counts + hit.astype(jnp.float32)
    blank = jnp.zeros((row_count, D), jnp.float32)
    blank_tail = (
        jnp.zeros((row_count, D), jnp.bfloat16),
        jnp.zeros((row_count, HEADS), jnp.float32),
        jnp.zeros((row_count, D), jnp.float32),
        jnp.zeros((row_count, D), jnp.bfloat16),
        jnp.zeros((row_count, FF), jnp.float32),
        jnp.zeros((row_count, FF), jnp.bfloat16),
    )
    inputs_kept = []
    tails_kept = []
    outputs = []
    input_grads = [blank]
    arriving = jnp.zeros((row_count, D), jnp.bfloat16)
    returning = jnp.zeros((row_count, D), jnp.bfloat16)
    layer_sums = tuple((jnp.zeros(member.shape, jnp.float32) for member in weights[2:]))
    modulation_grads = []

    def pick_embed(position):
        return sigma_embed[jnp.clip(position, 0, MICRO - 1)]

    for moment in range(MICRO + 2):
        if moment <= MICRO:
            fresh_rows = features[moment] if moment < MICRO else blank
            layer_in = jnp.where(first_section, fresh_rows, arriving.astype(jnp.float32))
            modulation = make_modulation(weights, pick_embed(moment - section_index))
            rim_parts = pre_attention(layer_in, modulation, weights)
            output, tail_parts = layer_tail(
                layer_in, modulation, weights, rim_parts, counts
            )
            inputs_kept.append(layer_in)
            tails_kept.append(tail_parts)
            outputs.append(output)
            if moment < MICRO:
                arriving = shifted(output.astype(jnp.bfloat16), "section", 1)
        if moment >= 1:
            position = moment - 2 + section_index
            layer_in = jnp.where(
                first_section,
                recall(inputs_kept, moment - 2, blank),
                recall(inputs_kept, moment, blank),
            )
            embed_row = pick_embed(position)
            modulation = make_modulation(weights, embed_row)
            rim_parts = pre_attention(layer_in, modulation, weights)
            lower_tail = recall(tails_kept, moment - 2, blank_tail)
            upper_tail = recall(tails_kept, moment, blank_tail)
            tail_parts = tuple(
                (
                    jnp.where(first_section, below, above)
                    for below, above in zip(lower_tail, upper_tail)
                )
            )
            sent_down = cotangent[moment - 1] if moment <= MICRO else blank
            grad_out = jnp.where(first_section, returning.astype(jnp.float32), sent_down)
            grad_in, grad_mod, layer_grads = layer_backward(
                layer_in, modulation, weights, rim_parts, tail_parts, counts, grad_out
            )
            input_grads.append(grad_in)
            if moment <= MICRO:
                returning = shifted(grad_in.astype(jnp.bfloat16), "section", -1)
            layer_sums = tuple(
                (running + addend for running, addend in zip(layer_sums, layer_grads))
            )
            modulation_grads.append(grad_mod)
    boundary = jnp.stack(
        [
            jnp.where(first_section, input_grads[position + 2], outputs[position + 1])
            for position in range(MICRO)
        ]
    )
    modulation_parts = jnp.stack(
        [
            jnp.where(first_section, modulation_grads[position + 1], modulation_grads[position])
            for position in range(MICRO)
        ]
    )
    modulation_sums, up_bias_sum, down_bias_sum = lax.psum(
        (modulation_parts, layer_sums[3], layer_sums[5]), "wide"
    )
    summed = lax.psum(
        tuple(layer_sums[k].astype(jnp.bfloat16) for k in (0, 1, 2, 4)), "wide"
    )
    summed = tuple(member.astype(jnp.float32) for member in summed)
    grad_ada_weight = jnp.sum(
        sigma_embed.astype(jnp.float32)[:, :, None] * modulation_sums[:, None, :], axis=0
    )
    grad_ada_bias = jnp.sum(modulation_sums, axis=0)
    remaining = (summed[0], summed[1], summed[2], up_bias_sum, summed[3], down_bias_sum)
    return (
        boundary[None],
        grad_ada_weight[None],
        grad_ada_bias[None],
        remaining[0][None],
        remaining[1][None],
        remaining[2][None],
        remaining[3][None],
        remaining[4][None],
        remaining[5][None],
    )


def solution(mesh):
    return jax.shard_map(
        shards,
        mesh=mesh,
        in_specs=(
            P(None, "wide", None),
            P(),
            P(None, "wide", None),
            P("wide", None),
            P("wide", None),
            P("section", None, None),
            P("section", None),
            P("section", None, None),
            P("section", None, None),
            P("section", None, None),
            P("section", None),
            P("section", None, None),
            P("section", None),
        ),
        out_specs=(
            P("section", None, "wide", None),
            P("section", None, None),
            P("section", None),
            P("section", None, None),
            P("section", None, None),
            P("section", None, None),
            P("section", None),
            P("section", None, None),
            P("section", None),
        ),
        check_vma=False,
    )
```

```python
import functools
import math

import jax
import jax.numpy as jnp
from jax import lax
from jax.experimental import pallas as pl
from jax.experimental.pallas import tpu as pltpu
from jax.sharding import PartitionSpec as P

D = 512
FF = 2048
HEADS = 4
HEAD_DIM = 128
NEIGHBOURS = 16
MICRO = 2
GRAD_ROWS = 12 * D
SMALL_ROWS = 16

norm_epsilon = 1e-05
masked_score = -1e30
LOG2E = math.log2(math.e)
SCORE_SCALE = HEAD_DIM**-0.5

MESH = pl.DeviceIdType.MESH
BF16 = jnp.bfloat16
F32 = jnp.float32


def mm(left, right):
    return jnp.dot(left, right, preferred_element_type=F32)


def mm_nt(left, right):
    return lax.dot_general(left, right, (((1,), (1,)), ((), ())), preferred_element_type=F32)


def mm_tn(left, right):
    return lax.dot_general(left, right, (((0,), (0,)), ((), ())), preferred_element_type=F32)


def row_mean(values):
    return jnp.mean(values, axis=-1, keepdims=True)


def normalize(values):
    center = values - row_mean(values)
    inverse = lax.rsqrt(row_mean(center * center) + norm_epsilon)
    return center * inverse, inverse


def column_sum(values):
    return jnp.sum(values, axis=0, keepdims=True)


def layer_kernel(
    sections,
    wide,
    features,
    cotangent,
    sigma,
    neighbours,
    valid_slots,
    ada_weight,
    ada_bias,
    qkv_weight,
    out_weight,
    up_weight,
    up_bias,
    down_weight,
    down_bias,
    boundary,
    grad_qkv_out,
    grad_out_out,
    grad_up_out,
    grad_down_out,
    small_out,
    w_qkv,
    w_out,
    w_up,
    w_down,
    mod,
    bias,
    x_in,
    g_out,
    near,
    query,
    key_value,
    attended,
    log_sum,
    mixed,
    normed_b,
    active,
    slope,
    grad_hidden,
    grad_low,
    grad_mixed_low,
    grad_query,
    grad_kv,
    grad_near,
    sent_near,
    back_near,
    sent_x,
    arrived_x,
    final_out,
    grads,
    landing,
    gathered,
    small,
    small_landing,
    load_sem,
    store_sem,
    halo_send,
    halo_recv,
    back_send,
    back_recv,
    x_send,
    x_recv,
    ring_send,
    ring_recv,
    small_send,
    small_recv,
):
    sec = lax.axis_index("section")
    me = lax.axis_index("wide")
    rows = x_in.shape[1]
    window = 3 * rows
    levels = wide.bit_length() - 1
    left = lax.rem(me + wide - 1, wide)
    right = lax.rem(me + 1, wide)
    first = sec == 0
    second = sec == 1

    def bit_of(level):
        return lax.rem(lax.div(me, 1 << level), 2)

    def partner(level):
        return me + (1 - 2 * bit_of(level)) * (1 << level)

    loads = []

    def load(source, target):
        copy = pltpu.make_async_copy(source, target, load_sem.at[len(loads)])
        loads.append(copy)
        return copy

    feature_loads = [load(features.at[m], x_in.at[m]) for m in range(MICRO)]
    ada_loads = [
        load(ada_weight.at[0, :, pl.ds(j * D, D)], gathered.at[pl.ds(j * D, D)]) for j in range(4)
    ]
    qkv_load = load(qkv_weight.at[0], w_qkv)
    out_load = load(out_weight.at[0], w_out)
    up_load = load(up_weight.at[0], w_up)
    down_load = load(down_weight.at[0], w_down)
    cotangent_loads = [load(cotangent.at[m], g_out.at[m]) for m in range(MICRO)]

    @pl.when(first)
    def _():
        for copy in feature_loads:
            copy.start()

    for copy in ada_loads:
        copy.start()
    for copy in (qkv_load, out_load, up_load, down_load):
        copy.start()

    @pl.when(second)
    def _():
        for copy in cotangent_loads:
            copy.start()

    barrier = pltpu.get_barrier_semaphore()
    peers = [(sec, left), (sec, right), (1 - sec, me)] + [
        (sec, partner(level)) for level in range(levels)
    ]
    for peer in peers:
        pl.semaphore_signal(barrier, inc=1, device_id=peer, device_id_type=MESH)

    start = (me - 1) * rows
    total_nodes = rows * wide

    block = 32

    @pl.loop(0, rows // block)
    def _(step):
        here = pl.ds(pl.multiple_of(step * block, block), block)
        places = neighbours[here, :] - start
        places = jnp.where(places >= total_nodes, places - total_nodes, places)
        places = jnp.where(places < 0, places + total_nodes, places)
        places = jnp.where(valid_slots[here, :] > 0, places, -1)
        columns = lax.broadcasted_iota(jnp.int32, (block, window), 1)
        counts = jnp.zeros((block, window), F32)
        for slot in range(NEIGHBOURS):
            counts += jnp.where(places[:, slot : slot + 1] == columns, 1.0, 0.0)
        bias[here, :] = jnp.where(counts > 0, jnp.log2(jnp.maximum(counts, 1.0)), masked_score)

    for j, copy in enumerate(ada_loads):
        copy.wait()
        mod[:, j * D : (j + 1) * D] = (
            mm(sigma[...], gathered[j * D : (j + 1) * D]) + ada_bias[:, j * D : (j + 1) * D]
        )

    pl.semaphore_wait(barrier, len(peers))

    def modulation(m, part):
        return mod[m : m + 1, part * D : (part + 1) * D]

    def halo_copy(m, side):
        base = m * window
        return pltpu.make_async_remote_copy(
            src_ref=near.at[pl.ds(base + rows, rows)],
            dst_ref=near.at[pl.ds(base + 2 * rows * side, rows)],
            send_sem=halo_send.at[m, side],
            recv_sem=halo_recv.at[m, side],
            device_id=(sec, left if side else right),
            device_id_type=MESH,
        )

    def back_copy(m, side):
        return pltpu.make_async_remote_copy(
            src_ref=sent_near.at[m, side],
            dst_ref=back_near.at[m, side],
            send_sem=back_send.at[m, side],
            recv_sem=back_recv.at[m, side],
            device_id=(sec, right if side else left),
            device_id_type=MESH,
        )

    def x_copy(m):
        return pltpu.make_async_remote_copy(
            src_ref=sent_x.at[m],
            dst_ref=arrived_x.at[m],
            send_sem=x_send.at[m],
            recv_sem=x_recv.at[m],
            device_id=(1 - sec, me),
            device_id_type=MESH,
        )

    def prepare(m):
        @pl.when(first)
        def _():
            feature_loads[m].wait()

        @pl.when(second)
        def _():
            x_copy(m).wait_recv()
            x_in[m] = arrived_x[m].astype(F32)

        unit, _ = normalize(x_in[m])
        own = pl.ds(m * window + rows, rows)
        near[own, :] = (unit * (1.0 + modulation(m, 1)) + modulation(m, 0)).astype(BF16)
        for side in range(2):
            halo_copy(m, side).start()

    def forward(m):
        base = m * window
        own = near[base + rows : base + 2 * rows]
        if m == 0:
            qkv_load.wait()
        query[m] = (mm(own, w_qkv[:, :D]) * (SCORE_SCALE * LOG2E)).astype(BF16)
        key_value[base + rows : base + 2 * rows] = mm(own, w_qkv[:, D:]).astype(BF16)
        for side in range(2):
            halo_copy(m, side).wait_recv()
            place = base + 2 * rows * side
            key_value[place : place + rows] = mm(near[place : place + rows], w_qkv[:, D:]).astype(
                BF16
            )
        for h in range(HEADS):
            low, high = h * HEAD_DIM, (h + 1) * HEAD_DIM
            scores = mm_nt(query[m, :, low:high], key_value[base : base + window, low:high])
            scores += bias[...]
            top = jnp.max(scores, axis=1, keepdims=True)
            raised = jnp.exp2(scores - top)
            total = jnp.sum(raised, axis=1, keepdims=True)
            part = mm(raised.astype(BF16), key_value[base : base + window, D + low : D + high])
            attended[m * rows : (m + 1) * rows, low:high] = (part / total).astype(BF16)
            log_sum[m, h] = top + jnp.log2(total)
        mine = slice(m * rows, (m + 1) * rows)
        if m == 0:
            for copy in (out_load, up_load, down_load):
                copy.wait()
        middle = x_in[m] + mm(attended[mine], w_out[...])
        mixed[m] = middle
        unit, _ = normalize(middle)
        normed_b[mine] = (unit * (1.0 + modulation(m, 3)) + modulation(m, 2)).astype(BF16)
        for j in range(FF // D):
            part = slice(j * D, (j + 1) * D)
            hidden = mm(normed_b[mine], w_up[:, part]) + up_bias[:, part]
            gate = 0.5 + 0.5 * jnp.tanh(0.5 * hidden)
            swish = hidden * gate
            active[mine, part] = swish.astype(BF16)
            slope[mine, part] = (gate + swish * (1.0 - gate)).astype(BF16)
        output = mixed[m] + mm(active[mine], w_down[...]) + down_bias[...]

        @pl.when(first)
        def _():
            sent_x[m] = output.astype(BF16)
            x_copy(m).start()

        @pl.when(second)
        def _():
            final_out[m] = output
            pltpu.make_async_copy(final_out.at[m], boundary.at[0, m], store_sem.at[m]).start()

    def backward(m):
        base = m * window
        mine = slice(m * rows, (m + 1) * rows)

        @pl.when(first)
        def _():
            x_copy(m).wait_recv()
            g_out[m] = arrived_x[m].astype(F32)

        @pl.when(second)
        def _():
            cotangent_loads[m].wait()

        grad_out = g_out[m]
        grad_low[mine] = grad_out.astype(BF16)
        down_sum = column_sum(grad_out)
        small[12:13] = down_sum if m == 0 else small[12:13] + down_sum
        for j in range(FF // D):
            part = slice(j * D, (j + 1) * D)
            hidden = mm_nt(grad_low[mine], w_down[part]) * slope[mine, part].astype(F32)
            hidden = hidden.astype(BF16)
            grad_hidden[mine, part] = hidden
            up_sum = column_sum(hidden.astype(F32))
            small[8 + j : 9 + j] = up_sum if m == 0 else small[8 + j : 9 + j] + up_sum
        grad_normed = mm_nt(grad_hidden[mine], w_up[...])
        unit, inverse = normalize(mixed[m])
        small[4 * m + 2 : 4 * m + 3] = column_sum(grad_normed)
        small[4 * m + 3 : 4 * m + 4] = column_sum(grad_normed * unit)
        scaled = grad_normed * (1.0 + modulation(m, 3))
        grad_mixed = g_out[m] + inverse * (
            scaled - row_mean(scaled) - unit * row_mean(scaled * unit)
        )
        mixed[m] = grad_mixed
        grad_mixed_low[mine] = grad_mixed.astype(BF16)
        grad_attended = mm_nt(grad_mixed_low[mine], w_out[...]).astype(BF16)
        for h in range(HEADS):
            low, high = h * HEAD_DIM, (h + 1) * HEAD_DIM
            queries = query[m, :, low:high]
            keys = key_value[base : base + window, low:high]
            values = key_value[base : base + window, D + low : D + high]
            grad = grad_attended[:, low:high]
            soft = jnp.exp2(mm_nt(queries, keys) + bias[...] - log_sum[m, h])
            grad_soft = mm_nt(grad, values)
            product = soft * grad_soft
            grad_scores = product - soft * jnp.sum(product, axis=1, keepdims=True)
            grad_scores = grad_scores.astype(BF16)
            grad_query[mine, low:high] = (mm(grad_scores, keys) * SCORE_SCALE).astype(BF16)
            grad_kv[base : base + window, low:high] = (
                mm_tn(grad_scores, queries) * (1.0 / LOG2E)
            ).astype(BF16)
            grad_kv[base : base + window, D + low : D + high] = mm_tn(
                soft.astype(BF16), grad
            ).astype(BF16)
        for side in range(2):
            place = base + 2 * rows * side
            sent_near[m, side] = mm_nt(grad_kv[place : place + rows], w_qkv[:, D:]).astype(BF16)
            back_copy(m, side).start()
        grad_near[m] = mm_nt(grad_query[mine], w_qkv[:, :D]) + mm_nt(
            grad_kv[base + rows : base + 2 * rows], w_qkv[:, D:]
        )

    def finish(m):
        for side in range(2):
            back_copy(m, side).wait_recv()
        grad_normed = (
            grad_near[m] + back_near[m, 0].astype(F32) + back_near[m, 1].astype(F32)
        )
        unit, inverse = normalize(x_in[m])
        small[4 * m : 4 * m + 1] = column_sum(grad_normed)
        small[4 * m + 1 : 4 * m + 2] = column_sum(grad_normed * unit)
        scaled = grad_normed * (1.0 + modulation(m, 1))
        grad_in = mixed[m] + inverse * (
            scaled - row_mean(scaled) - unit * row_mean(scaled * unit)
        )

        @pl.when(second)
        def _():
            sent_x[m] = grad_in.astype(BF16)
            x_copy(m).start()

        @pl.when(first)
        def _():
            final_out[m] = grad_in
            pltpu.make_async_copy(final_out.at[m], boundary.at[0, m], store_sem.at[m]).start()

    def weight_grad(block):
        if block < 4:
            value = mm_tn(active[:, block * D : (block + 1) * D], grad_low[...])
        elif block < 8:
            value = mm_tn(normed_b[...], grad_hidden[:, (block - 4) * D : (block - 3) * D])
        elif block == 8:
            value = mm_tn(attended[...], grad_mixed_low[...])
        elif block == 9:
            value = sum(
                mm_tn(
                    near[m * window + rows : m * window + 2 * rows],
                    grad_query[m * rows : (m + 1) * rows],
                )
                for m in range(MICRO)
            )
        else:
            value = mm_tn(near[...], grad_kv[:, (block - 10) * D : (block - 9) * D])
        grads[block * D : (block + 1) * D] = value.astype(BF16)

    def block_target(block):
        if block < 4:
            return grad_down_out.at[pl.ds(block * D, D)]
        if block < 8:
            return grad_up_out.at[:, pl.ds((block - 4) * D, D)]
        if block == 8:
            return grad_out_out
        return grad_qkv_out.at[:, pl.ds((block - 9) * D, D)]

    task_rows = max(D, 16 * wide)
    tasks = GRAD_ROWS // task_rows
    per_task = task_rows // D

    def order(task):
        return list(range(levels))

    def segment(task, stage):
        base = task * task_rows
        size = task_rows
        for level in order(task)[:stage]:
            size //= 2
            base = base + bit_of(level) * size
        return base, size

    def halving(task, stage):
        level = order(task)[stage]
        base, size = segment(task, stage)
        half = size // 2
        away = pl.multiple_of(base + (1 - bit_of(level)) * half, 16)
        spot = task * task_rows + task_rows - size
        return pltpu.make_async_remote_copy(
            src_ref=grads.at[pl.ds(away, half)],
            dst_ref=landing.at[pl.ds(spot, half)],
            send_sem=ring_send.at[task, stage],
            recv_sem=ring_recv.at[task, stage],
            device_id=(sec, partner(level)),
            device_id_type=MESH,
        )

    def doubling(task, stage):
        level = order(task)[levels - 1 - stage]
        base, size = segment(task, levels - stage)
        place = pl.ds(pl.multiple_of(base, 16), size)
        return pltpu.make_async_remote_copy(
            src_ref=gathered.at[place],
            dst_ref=gathered.at[place],
            send_sem=ring_send.at[task, levels + stage],
            recv_sem=ring_recv.at[task, levels + stage],
            device_id=(sec, partner(level)),
            device_id_type=MESH,
        )

    def reduce_step(task, stage):
        if stage == 0:
            halving(task, 0).start()
            return
        if stage <= levels:
            halving(task, stage - 1).wait_recv()
            base, size = segment(task, stage)
            spot = task * task_rows + task_rows - 2 * size
            place = pl.ds(pl.multiple_of(base, 16), size)
            value = grads[place, :].astype(F32) + landing[spot : spot + size].astype(F32)
            if stage < levels:
                grads[place, :] = value.astype(BF16)
                halving(task, stage).start()
            else:
                gathered[place, :] = value.astype(BF16)
                doubling(task, 0).start()
            return
        doubling(task, stage - levels - 1).wait_recv()
        if stage < 2 * levels:
            doubling(task, stage - levels).start()
        else:
            for block in range(task * per_task, (task + 1) * per_task):
                pltpu.make_async_copy(
                    gathered.at[pl.ds(block * D, D)], block_target(block), store_sem.at[2 + block]
                ).start()

    def small_copy(level):
        return pltpu.make_async_remote_copy(
            src_ref=small.at[pl.ds(0, SMALL_ROWS)] if level == 0 else small_landing.at[1, level],
            dst_ref=small_landing.at[0, level],
            send_sem=small_send.at[level],
            recv_sem=small_recv.at[level],
            device_id=(sec, partner(level)),
            device_id_type=MESH,
        )

    def small_step(level):
        if level > 0:
            small_copy(level - 1).wait_recv()
            held = small[...] if level == 1 else small_landing[1, level - 1]
            value = held + small_landing[0, level - 1]
            if level == levels:
                small_landing[1, 0] = value
                return
            small_landing[1, level] = value
        small_copy(level).start()

    small[13:SMALL_ROWS] = jnp.zeros((SMALL_ROWS - 13, D), F32)
    for m in range(MICRO):
        prepare(m)
    for m in range(MICRO):
        forward(m)

    @pl.when(first)
    def _():
        for m in range(MICRO):
            x_copy(m).wait_send()

    for m in range(MICRO):
        backward(m)
    for m in range(MICRO):
        finish(m)
    for block in range(12):
        weight_grad(block)
    small_step(0)
    last = 2 * levels
    for moment in range(tasks + last):
        for stage in range(last, -1, -1):
            task = moment - stage
            if 0 <= task < tasks:
                reduce_step(task, stage)
        if 1 <= moment <= levels:
            small_step(moment)
    small_out[...] = small_landing[1, 0]

    for m in range(MICRO):
        for side in range(2):
            halo_copy(m, side).wait_send()
            back_copy(m, side).wait_send()
        pltpu.make_async_copy(final_out.at[m], boundary.at[0, m], store_sem.at[m]).wait()

    @pl.when(second)
    def _():
        for m in range(MICRO):
            x_copy(m).wait_send()

    for task in range(tasks):
        for stage in range(levels):
            halving(task, stage).wait_send()
            doubling(task, stage).wait_send()
    for level in range(levels):
        small_copy(level).wait_send()
    for block in range(12):
        pltpu.make_async_copy(
            gathered.at[pl.ds(block * D, D)], block_target(block), store_sem.at[2 + block]
        ).wait()


def shards(
    features,
    sigma_embed,
    cotangent,
    neighbours,
    valid_slots,
    ada_weight,
    ada_bias,
    qkv_weight,
    out_weight,
    up_weight,
    up_bias,
    down_weight,
    down_bias,
):
    rows = features.shape[1]
    wide = lax.axis_size("wide")
    sections = lax.axis_size("section")
    levels = wide.bit_length() - 1
    tasks = GRAD_ROWS // max(D, 16 * wide)
    window = 3 * rows
    every = pl.BlockSpec(memory_space=pl.ANY)
    vmem = pl.BlockSpec(memory_space=pltpu.VMEM)
    dma = pltpu.SemaphoreType.DMA
    outs = pl.pallas_call(
        functools.partial(layer_kernel, sections, wide),
        out_shape=(
            jax.ShapeDtypeStruct((1, MICRO, rows, D), F32),
            jax.ShapeDtypeStruct((D, 3 * D), BF16),
            jax.ShapeDtypeStruct((D, D), BF16),
            jax.ShapeDtypeStruct((D, FF), BF16),
            jax.ShapeDtypeStruct((FF, D), BF16),
            jax.ShapeDtypeStruct((SMALL_ROWS, D), F32),
        ),
        in_specs=[every, every, vmem, vmem, vmem, every, vmem, every, every, every, vmem, every, vmem],
        out_specs=[every, every, every, every, every, vmem],
        scratch_shapes=[
            pltpu.VMEM((D, 3 * D), BF16),
            pltpu.VMEM((D, D), BF16),
            pltpu.VMEM((D, FF), BF16),
            pltpu.VMEM((FF, D), BF16),
            pltpu.VMEM((MICRO, 4 * D), F32),
            pltpu.VMEM((rows, window), F32),
            pltpu.VMEM((MICRO, rows, D), F32),
            pltpu.VMEM((MICRO, rows, D), F32),
            pltpu.VMEM((MICRO * window, D), BF16),
            pltpu.VMEM((MICRO, rows, D), BF16),
            pltpu.VMEM((MICRO * window, 2 * D), BF16),
            pltpu.VMEM((MICRO * rows, D), BF16),
            pltpu.VMEM((MICRO, HEADS, rows, 1), F32),
            pltpu.VMEM((MICRO, rows, D), F32),
            pltpu.VMEM((MICRO * rows, D), BF16),
            pltpu.VMEM((MICRO * rows, FF), BF16),
            pltpu.VMEM((MICRO * rows, FF), BF16),
            pltpu.VMEM((MICRO * rows, FF), BF16),
            pltpu.VMEM((MICRO * rows, D), BF16),
            pltpu.VMEM((MICRO * rows, D), BF16),
            pltpu.VMEM((MICRO * rows, D), BF16),
            pltpu.VMEM((MICRO * window, 2 * D), BF16),
            pltpu.VMEM((MICRO, rows, D), F32),
            pltpu.VMEM((MICRO, 2, rows, D), BF16),
            pltpu.VMEM((MICRO, 2, rows, D), BF16),
            pltpu.VMEM((MICRO, rows, D), BF16),
            pltpu.VMEM((MICRO, rows, D), BF16),
            pltpu.VMEM((MICRO, rows, D), F32),
            pltpu.VMEM((GRAD_ROWS, D), BF16),
            pltpu.VMEM((GRAD_ROWS, D), BF16),
            pltpu.VMEM((GRAD_ROWS, D), BF16),
            pltpu.VMEM((SMALL_ROWS, D), F32),
            pltpu.VMEM((2, levels, SMALL_ROWS, D), F32),
            dma((12,)),
            dma((2 + 12,)),
            dma((MICRO, 2)),
            dma((MICRO, 2)),
            dma((MICRO, 2)),
            dma((MICRO, 2)),
            dma((MICRO,)),
            dma((MICRO,)),
            dma((tasks, 2 * levels)),
            dma((tasks, 2 * levels)),
            dma((levels,)),
            dma((levels,)),
        ],
        compiler_params=pltpu.CompilerParams(
            collective_id=1, has_side_effects=True, vmem_limit_bytes=63 * 1024 * 1024
        ),
        name="layers",
    )(
        features,
        cotangent,
        sigma_embed,
        neighbours,
        valid_slots,
        ada_weight,
        ada_bias,
        qkv_weight,
        out_weight,
        up_weight,
        up_bias,
        down_weight,
        down_bias,
    )
    boundary, grad_qkv, grad_out, grad_up, grad_down, small = outs
    modulation_sums = small[: 4 * MICRO].reshape(MICRO, 4 * D)
    grad_ada_weight = jnp.sum(
        sigma_embed.astype(F32)[:, :, None] * modulation_sums[:, None, :], axis=0
    )
    grad_ada_bias = jnp.sum(modulation_sums, axis=0)
    return (
        boundary,
        grad_ada_weight[None],
        grad_ada_bias[None],
        grad_qkv.astype(F32)[None],
        grad_out.astype(F32)[None],
        grad_up.astype(F32)[None],
        small[8:12].reshape(1, FF),
        grad_down.astype(F32)[None],
        small[12:13].reshape(1, D),
    )


def solution(mesh):
    return jax.shard_map(
        shards,
        mesh=mesh,
        in_specs=(
            P(None, "wide", None),
            P(),
            P(None, "wide", None),
            P("wide", None),
            P("wide", None),
            P("section", None, None),
            P("section", None),
            P("section", None, None),
            P("section", None, None),
            P("section", None, None),
            P("section", None),
            P("section", None, None),
            P("section", None),
        ),
        out_specs=(
            P("section", None, "wide", None),
            P("section", None, None),
            P("section", None),
            P("section", None, None),
            P("section", None, None),
            P("section", None, None),
            P("section", None),
            P("section", None, None),
            P("section", None),
        ),
        check_vma=False,
    )
```

```python
import functools
import math

import jax
import jax.numpy as jnp
from jax import lax
from jax.experimental import pallas as pl
from jax.experimental.pallas import tpu as pltpu
from jax.sharding import PartitionSpec as P

D = 512
FF = 2048
HEADS = 4
HEAD_DIM = 128
NEIGHBOURS = 16
MICRO = 2
GRAD_ROWS = 12 * D
SMALL_ROWS = 16
CHUNKS = 4

norm_epsilon = 1e-05
masked_score = -1e30
LOG2E = math.log2(math.e)
SCORE_SCALE = HEAD_DIM**-0.5

MESH = pl.DeviceIdType.MESH
BF16 = jnp.bfloat16
F32 = jnp.float32


def mm(left, right):
    return jnp.dot(left, right, preferred_element_type=F32)


def mm_nt(left, right):
    return lax.dot_general(left, right, (((1,), (1,)), ((), ())), preferred_element_type=F32)


def mm_tn(left, right):
    return lax.dot_general(left, right, (((0,), (0,)), ((), ())), preferred_element_type=F32)


def row_mean(values):
    return jnp.mean(values, axis=-1, keepdims=True)


def normalize(values):
    center = values - row_mean(values)
    inverse = lax.rsqrt(row_mean(center * center) + norm_epsilon)
    return center * inverse, inverse


def column_sum(values):
    return jnp.sum(values, axis=0, keepdims=True)


def layer_kernel(
    sections,
    wide,
    features,
    cotangent,
    sigma,
    neighbours,
    valid_slots,
    ada_weight,
    ada_bias,
    qkv_weight,
    out_weight,
    up_weight,
    up_bias,
    down_weight,
    down_bias,
    boundary,
    grad_qkv_out,
    grad_out_out,
    grad_up_out,
    grad_down_out,
    small_out,
    w_qkv,
    w_out,
    w_up,
    w_down,
    mod,
    slots,
    bias,
    x_in,
    g_out,
    near,
    query,
    key_value,
    attended,
    log_sum,
    mixed,
    normed_b,
    active,
    slope,
    grad_hidden,
    grad_low,
    grad_mixed_low,
    grad_query,
    grad_kv,
    grad_attended,
    grad_near,
    sent_near,
    back_near,
    sent_x,
    arrived_x,
    grads,
    landing,
    gathered,
    small,
    small_landing,
    load_sem,
    store_sem,
    halo_send,
    halo_recv,
    back_send,
    back_recv,
    x_send,
    x_recv,
    ring_send,
    ring_recv,
    small_send,
    small_recv,
):
    sec = lax.axis_index("section")
    me = lax.axis_index("wide")
    rows = x_in.shape[1]
    window = 3 * rows
    levels = wide.bit_length() - 1
    left = lax.rem(me + wide - 1, wide)
    right = lax.rem(me + 1, wide)
    first = sec == 0
    second = sec == 1

    def bit_of(level):
        return lax.rem(lax.div(me, 1 << level), 2)

    def partner(level):
        return me + (1 - 2 * bit_of(level)) * (1 << level)

    loads = []

    def load(source, target):
        copy = pltpu.make_async_copy(source, target, load_sem.at[len(loads)])
        loads.append(copy)
        return copy

    feature_loads = [load(features.at[m], x_in.at[m]) for m in range(MICRO)]
    ada_loads = [
        load(ada_weight.at[0, :, pl.ds(j * D, D)], gathered.at[pl.ds(j * D, D)]) for j in range(4)
    ]
    qkv_load = load(qkv_weight.at[0], w_qkv)
    out_load = load(out_weight.at[0], w_out)
    up_load = load(up_weight.at[0], w_up)
    down_load = load(down_weight.at[0], w_down)
    cotangent_loads = [load(cotangent.at[m], g_out.at[m]) for m in range(MICRO)]

    @pl.when(first)
    def _():
        for copy in feature_loads:
            copy.start()

    for copy in ada_loads:
        copy.start()
    for copy in (qkv_load, out_load, up_load, down_load):
        copy.start()

    @pl.when(second)
    def _():
        for copy in cotangent_loads:
            copy.start()

    barrier = pltpu.get_barrier_semaphore()
    peers = [(sec, left), (sec, right), (1 - sec, me)] + [
        (sec, partner(level)) for level in range(levels)
    ]
    for peer in peers:
        pl.semaphore_signal(barrier, inc=1, device_id=peer, device_id_type=MESH)

    def count_slots():
        start = (me - 1) * rows
        total_nodes = rows * wide
        offsets = neighbours[...] - start
        offsets = jnp.where(offsets >= total_nodes, offsets - total_nodes, offsets)
        offsets = jnp.where(offsets < 0, offsets + total_nodes, offsets)
        offsets = jnp.where(valid_slots[...] > 0, offsets, -1)
        slots[...] = jnp.transpose(offsets.astype(F32))
        block = 32

        @pl.loop(0, rows // block)
        def _(step):
            here = pl.ds(pl.multiple_of(step * block, block), block)
            places = slots[here, :].astype(jnp.int32)
            columns = lax.broadcasted_iota(jnp.int32, (block, window), 1)
            counts = jnp.zeros((block, window), F32)
            for slot in range(NEIGHBOURS):
                counts += jnp.where(places[:, slot : slot + 1] == columns, 1.0, 0.0)
            bias[here, :] = jnp.where(
                counts > 0, jnp.log2(jnp.maximum(counts, 1.0)), masked_score
            )

    for j, copy in enumerate(ada_loads):
        copy.wait()
        mod[:, j * D : (j + 1) * D] = (
            mm(sigma[...], gathered[j * D : (j + 1) * D]) + ada_bias[:, j * D : (j + 1) * D]
        )

    pl.semaphore_wait(barrier, len(peers))

    def modulation(m, part):
        return mod[m : m + 1, part * D : (part + 1) * D]

    chunk = rows // CHUNKS

    def halo_copy(m, side, c):
        base = m * window + c * chunk
        return pltpu.make_async_remote_copy(
            src_ref=near.at[pl.ds(base + rows, chunk)],
            dst_ref=near.at[pl.ds(base + 2 * rows * side, chunk)],
            send_sem=halo_send.at[m, side, c],
            recv_sem=halo_recv.at[m, side, c],
            device_id=(sec, left if side else right),
            device_id_type=MESH,
        )

    def back_copy(m, side, c):
        part = pl.ds(c * chunk, chunk)
        return pltpu.make_async_remote_copy(
            src_ref=sent_near.at[m, side, part],
            dst_ref=back_near.at[m, side, part],
            send_sem=back_send.at[m, side, c],
            recv_sem=back_recv.at[m, side, c],
            device_id=(sec, right if side else left),
            device_id_type=MESH,
        )

    def x_copy(m, c):
        part = pl.ds(c * chunk, chunk)
        return pltpu.make_async_remote_copy(
            src_ref=sent_x.at[m, part],
            dst_ref=arrived_x.at[m, part],
            send_sem=x_send.at[m, c],
            recv_sem=x_recv.at[m, c],
            device_id=(1 - sec, me),
            device_id_type=MESH,
        )

    def final_copy(m):
        return pltpu.make_async_copy(grad_near.at[m], boundary.at[0, m], store_sem.at[m])

    def grad_copy(m):
        return pltpu.make_async_copy(mixed.at[m], boundary.at[0, m], store_sem.at[m])

    def start_halo(m, c):
        for side in range(2):
            halo_copy(m, side, c).start()

    def prepare(m, arriving, send):
        if not arriving:
            feature_loads[m].wait()
        for c in range(CHUNKS):
            part = slice(c * chunk, (c + 1) * chunk)
            if arriving:
                x_copy(m, c).wait_recv()
                x_in[m, part] = arrived_x[m, part].astype(F32)
            unit, _ = normalize(x_in[m, part])
            own = pl.ds(m * window + rows + c * chunk, chunk)
            near[own, :] = (unit * (1.0 + modulation(m, 1)) + modulation(m, 0)).astype(BF16)
            if send:
                start_halo(m, c)

    def forward(m):
        base = m * window
        own = near[base + rows : base + 2 * rows]
        if m == 0:
            qkv_load.wait()
        query[m] = (mm(own, w_qkv[:, :D]) * (SCORE_SCALE * LOG2E)).astype(BF16)
        key_value[base + rows : base + 2 * rows] = mm(own, w_qkv[:, D:]).astype(BF16)
        for side in range(2):
            for c in range(CHUNKS):
                halo_copy(m, side, c).wait_recv()
        if m == 0:
            for c in range(CHUNKS):
                start_halo(1, c)
        for side in range(2):
            place = base + 2 * rows * side
            key_value[place : place + rows] = mm(near[place : place + rows], w_qkv[:, D:]).astype(
                BF16
            )
        for h in range(HEADS):
            low, high = h * HEAD_DIM, (h + 1) * HEAD_DIM
            scores = mm_nt(query[m, :, low:high], key_value[base : base + window, low:high])
            scores += bias[...]
            top = jnp.max(scores, axis=1, keepdims=True)
            raised = jnp.exp2(scores - top)
            total = jnp.sum(raised, axis=1, keepdims=True)
            part = mm(raised.astype(BF16), key_value[base : base + window, D + low : D + high])
            attended[m * rows : (m + 1) * rows, low:high] = (part / total).astype(BF16)
            log_sum[m, :, h : h + 1] = top + jnp.log2(total)
        mine = slice(m * rows, (m + 1) * rows)
        if m == 0:
            for copy in (out_load, up_load, down_load):
                copy.wait()
        middle = x_in[m] + mm(attended[mine], w_out[...])
        mixed[m] = middle
        unit, _ = normalize(middle)
        normed_b[mine] = (unit * (1.0 + modulation(m, 3)) + modulation(m, 2)).astype(BF16)
        for j in range(FF // D):
            part = slice(j * D, (j + 1) * D)
            hidden = mm(normed_b[mine], w_up[:, part]) + up_bias[:, part]
            gate = 0.5 + 0.5 * jnp.tanh(0.5 * hidden)
            swish = hidden * gate
            active[mine, part] = swish.astype(BF16)
            slope[mine, part] = (gate + swish * (1.0 - gate)).astype(BF16)
        output = mixed[m] + mm(active[mine], w_down[...]) + down_bias[...]

        @pl.when(first)
        def _():
            for c in range(CHUNKS):
                part = slice(c * chunk, (c + 1) * chunk)
                sent_x[m, part] = output[part].astype(BF16)
                x_copy(m, c).start()

        @pl.when(second)
        def _():
            grad_near[m] = output
            final_copy(m).start()

    def backward_dense(m):
        mine = slice(m * rows, (m + 1) * rows)

        @pl.when(first)
        def _():
            for c in range(CHUNKS):
                x_copy(m, c).wait_recv()
            g_out[m] = arrived_x[m].astype(F32)

        @pl.when(second)
        def _():
            cotangent_loads[m].wait()

        grad_out = g_out[m]
        grad_low[mine] = grad_out.astype(BF16)
        down_sum = column_sum(grad_out)
        small[12:13] = down_sum if m == 0 else small[12:13] + down_sum
        for j in range(FF // D):
            part = slice(j * D, (j + 1) * D)
            hidden = mm_nt(grad_low[mine], w_down[part]) * slope[mine, part].astype(F32)
            hidden = hidden.astype(BF16)
            grad_hidden[mine, part] = hidden
            up_sum = column_sum(hidden.astype(F32))
            small[8 + j : 9 + j] = up_sum if m == 0 else small[8 + j : 9 + j] + up_sum
        grad_normed = mm_nt(grad_hidden[mine], w_up[...])
        unit, inverse = normalize(mixed[m])
        small[4 * m + 2 : 4 * m + 3] = column_sum(grad_normed)
        small[4 * m + 3 : 4 * m + 4] = column_sum(grad_normed * unit)
        scaled = grad_normed * (1.0 + modulation(m, 3))
        grad_mixed = g_out[m] + inverse * (
            scaled - row_mean(scaled) - unit * row_mean(scaled * unit)
        )
        mixed[m] = grad_mixed
        grad_mixed_low[mine] = grad_mixed.astype(BF16)
        grad_attended[...] = mm_nt(grad_mixed_low[mine], w_out[...]).astype(BF16)

    def backward_heads(m, heads):
        base = m * window
        mine = slice(m * rows, (m + 1) * rows)
        for h in heads:
            low, high = h * HEAD_DIM, (h + 1) * HEAD_DIM
            queries = query[m, :, low:high]
            keys = key_value[base : base + window, low:high]
            values = key_value[base : base + window, D + low : D + high]
            grad = grad_attended[:, low:high]
            soft = jnp.exp2(mm_nt(queries, keys) + bias[...] - log_sum[m, :, h : h + 1])
            grad_soft = mm_nt(grad, values)
            product = soft * grad_soft
            grad_scores = product - soft * jnp.sum(product, axis=1, keepdims=True)
            grad_scores = grad_scores.astype(BF16)
            grad_query[mine, low:high] = (mm(grad_scores, keys) * SCORE_SCALE).astype(BF16)
            grad_kv[base : base + window, low:high] = (
                mm_tn(grad_scores, queries) * (1.0 / LOG2E)
            ).astype(BF16)
            grad_kv[base : base + window, D + low : D + high] = mm_tn(
                soft.astype(BF16), grad
            ).astype(BF16)

    def send_back(m):
        base = m * window
        mine = slice(m * rows, (m + 1) * rows)
        for side in range(2):
            place = base + 2 * rows * side
            sent_near[m, side] = mm_nt(grad_kv[place : place + rows], w_qkv[:, D:]).astype(BF16)
        for c in range(CHUNKS):
            for side in range(2):
                back_copy(m, side, c).start()

        @pl.when(second)
        def _():
            final_copy(m).wait()

        grad_near[m] = mm_nt(grad_query[mine], w_qkv[:, :D]) + mm_nt(
            grad_kv[base + rows : base + 2 * rows], w_qkv[:, D:]
        )

    def finish(m, returning):
        shift_sum = jnp.zeros((1, D), F32)
        scale_sum = jnp.zeros((1, D), F32)
        for c in range(CHUNKS):
            part = slice(c * chunk, (c + 1) * chunk)
            for side in range(2):
                back_copy(m, side, c).wait_recv()
            grad_normed = (
                grad_near[m, part]
                + back_near[m, 0, part].astype(F32)
                + back_near[m, 1, part].astype(F32)
            )
            unit, inverse = normalize(x_in[m, part])
            scaled = grad_normed * (1.0 + modulation(m, 1))
            grad_in = mixed[m, part] + inverse * (
                scaled - row_mean(scaled) - unit * row_mean(scaled * unit)
            )
            if returning:
                sent_x[m, part] = grad_in.astype(BF16)
                x_copy(m, c).start()
            else:
                mixed[m, part] = grad_in
            shift_sum += column_sum(grad_normed)
            scale_sum += column_sum(grad_normed * unit)
        small[4 * m : 4 * m + 1] = shift_sum
        small[4 * m + 1 : 4 * m + 2] = scale_sum
        if not returning:
            grad_copy(m).start()

    def weight_grad(block):
        if block < 4:
            value = mm_tn(active[:, block * D : (block + 1) * D], grad_low[...])
        elif block < 8:
            value = mm_tn(normed_b[...], grad_hidden[:, (block - 4) * D : (block - 3) * D])
        elif block == 8:
            value = mm_tn(attended[...], grad_mixed_low[...])
        elif block == 9:
            value = sum(
                mm_tn(
                    near[m * window + rows : m * window + 2 * rows],
                    grad_query[m * rows : (m + 1) * rows],
                )
                for m in range(MICRO)
            )
        else:
            value = mm_tn(near[...], grad_kv[:, (block - 10) * D : (block - 9) * D])
        grads[block * D : (block + 1) * D] = value.astype(BF16)

    def block_target(block):
        if block < 4:
            return grad_down_out.at[pl.ds(block * D, D)]
        if block < 8:
            return grad_up_out.at[:, pl.ds((block - 4) * D, D)]
        if block == 8:
            return grad_out_out
        return grad_qkv_out.at[:, pl.ds((block - 9) * D, D)]

    task_rows = max(D, 16 * wide)
    tasks = GRAD_ROWS // task_rows
    per_task = task_rows // D

    def order(task):
        if task % 6 == 2 and levels > 2:
            return [0] + list(range(2, levels)) + [1]
        return list(range(levels))

    def segment(task, stage):
        base = task * task_rows
        size = task_rows
        for level in order(task)[:stage]:
            size //= 2
            base = base + bit_of(level) * size
        return base, size

    def halving(task, stage):
        level = order(task)[stage]
        base, size = segment(task, stage)
        half = size // 2
        away = pl.multiple_of(base + (1 - bit_of(level)) * half, 16)
        spot = task * task_rows + task_rows - size
        return pltpu.make_async_remote_copy(
            src_ref=grads.at[pl.ds(away, half)],
            dst_ref=landing.at[pl.ds(spot, half)],
            send_sem=ring_send.at[task, stage],
            recv_sem=ring_recv.at[task, stage],
            device_id=(sec, partner(level)),
            device_id_type=MESH,
        )

    def doubling(task, stage):
        level = order(task)[levels - 1 - stage]
        base, size = segment(task, levels - stage)
        place = pl.ds(pl.multiple_of(base, 16), size)
        return pltpu.make_async_remote_copy(
            src_ref=gathered.at[place],
            dst_ref=gathered.at[place],
            send_sem=ring_send.at[task, levels + stage],
            recv_sem=ring_recv.at[task, levels + stage],
            device_id=(sec, partner(level)),
            device_id_type=MESH,
        )

    def reduce_step(task, stage):
        if stage == 0:
            halving(task, 0).start()
            return
        if stage <= levels:
            halving(task, stage - 1).wait_recv()
            base, size = segment(task, stage)
            spot = task * task_rows + task_rows - 2 * size
            place = pl.ds(pl.multiple_of(base, 16), size)
            value = grads[place, :].astype(F32) + landing[spot : spot + size].astype(F32)
            if stage < levels:
                grads[place, :] = value.astype(BF16)
                halving(task, stage).start()
            else:
                gathered[place, :] = value.astype(BF16)
                doubling(task, 0).start()
            return
        doubling(task, stage - levels - 1).wait_recv()
        if stage < 2 * levels:
            doubling(task, stage - levels).start()
        else:
            for block in range(task * per_task, (task + 1) * per_task):
                pltpu.make_async_copy(
                    gathered.at[pl.ds(block * D, D)], block_target(block), store_sem.at[2 + block]
                ).start()

    def small_copy(level):
        return pltpu.make_async_remote_copy(
            src_ref=small.at[pl.ds(0, SMALL_ROWS)] if level == 0 else small_landing.at[1, level],
            dst_ref=small_landing.at[0, level],
            send_sem=small_send.at[level],
            recv_sem=small_recv.at[level],
            device_id=(sec, partner(level)),
            device_id_type=MESH,
        )

    def small_step(level):
        if level > 0:
            small_copy(level - 1).wait_recv()
            held = small[...] if level == 1 else small_landing[1, level - 1]
            value = held + small_landing[0, level - 1]
            if level == levels:
                small_landing[1, 0] = value
                return
            small_landing[1, level] = value
        small_copy(level).start()

    small[13:SMALL_ROWS] = jnp.zeros((SMALL_ROWS - 13, D), F32)

    @pl.when(first)
    def _():
        prepare(0, False, True)
        prepare(1, False, False)

    count_slots()

    @pl.when(second)
    def _():
        prepare(0, True, True)
        prepare(1, True, False)

    for m in range(MICRO):
        forward(m)

    @pl.when(first)
    def _():
        for m in range(MICRO):
            for c in range(CHUNKS):
                x_copy(m, c).wait_send()

    backward_dense(0)
    backward_heads(0, range(HEADS))
    send_back(0)
    backward_dense(1)

    @pl.when(second)
    def _():
        backward_heads(1, range(HEADS))
        send_back(1)
        finish(0, True)
        finish(1, True)

    extras = {2 + h: functools.partial(backward_heads, 1, [h]) for h in range(HEADS)}
    extras[6] = functools.partial(send_back, 1)
    extras[7] = functools.partial(finish, 0, False)
    extras[11] = functools.partial(finish, 1, False)

    offsets = [0, 1] + [2 * stage - 1 for stage in range(2, 2 * levels)] + [4 * levels - 2]
    for moment in range(tasks + offsets[-1]):
        if moment < tasks:
            for block in range(moment * per_task, (moment + 1) * per_task):
                if block in extras:
                    pl.when(first)(extras[block])
                weight_grad(block)
        for stage in range(2 * levels, -1, -1):
            task = moment - offsets[stage]
            if 0 <= task < tasks:
                reduce_step(task, stage)
        if 0 <= moment - tasks <= levels:
            small_step(moment - tasks)
    small_out[...] = small_landing[1, 0]

    for m in range(MICRO):
        for side in range(2):
            for c in range(CHUNKS):
                halo_copy(m, side, c).wait_send()
                back_copy(m, side, c).wait_send()

    @pl.when(first)
    def _():
        for m in range(MICRO):
            grad_copy(m).wait()

    @pl.when(second)
    def _():
        for m in range(MICRO):
            for c in range(CHUNKS):
                x_copy(m, c).wait_send()

    for task in range(tasks):
        for stage in range(levels):
            halving(task, stage).wait_send()
            doubling(task, stage).wait_send()
    for level in range(levels):
        small_copy(level).wait_send()
    for block in range(12):
        pltpu.make_async_copy(
            gathered.at[pl.ds(block * D, D)], block_target(block), store_sem.at[2 + block]
        ).wait()


def shards(
    features,
    sigma_embed,
    cotangent,
    neighbours,
    valid_slots,
    ada_weight,
    ada_bias,
    qkv_weight,
    out_weight,
    up_weight,
    up_bias,
    down_weight,
    down_bias,
):
    rows = features.shape[1]
    wide = lax.axis_size("wide")
    sections = lax.axis_size("section")
    levels = wide.bit_length() - 1
    tasks = GRAD_ROWS // max(D, 16 * wide)
    window = 3 * rows
    every = pl.BlockSpec(memory_space=pl.ANY)
    vmem = pl.BlockSpec(memory_space=pltpu.VMEM)
    dma = pltpu.SemaphoreType.DMA
    outs = pl.pallas_call(
        functools.partial(layer_kernel, sections, wide),
        out_shape=(
            jax.ShapeDtypeStruct((1, MICRO, rows, D), F32),
            jax.ShapeDtypeStruct((D, 3 * D), BF16),
            jax.ShapeDtypeStruct((D, D), BF16),
            jax.ShapeDtypeStruct((D, FF), BF16),
            jax.ShapeDtypeStruct((FF, D), BF16),
            jax.ShapeDtypeStruct((SMALL_ROWS, D), F32),
        ),
        in_specs=[every, every, vmem, vmem, vmem, every, vmem, every, every, every, vmem, every, vmem],
        out_specs=[every, every, every, every, every, vmem],
        scratch_shapes=[
            pltpu.VMEM((D, 3 * D), BF16),
            pltpu.VMEM((D, D), BF16),
            pltpu.VMEM((D, FF), BF16),
            pltpu.VMEM((FF, D), BF16),
            pltpu.VMEM((MICRO, 4 * D), F32),
            pltpu.VMEM((rows, NEIGHBOURS), F32),
            pltpu.VMEM((rows, window), F32),
            pltpu.VMEM((MICRO, rows, D), F32),
            pltpu.VMEM((MICRO, rows, D), F32),
            pltpu.VMEM((MICRO * window, D), BF16),
            pltpu.VMEM((MICRO, rows, D), BF16),
            pltpu.VMEM((MICRO * window, 2 * D), BF16),
            pltpu.VMEM((MICRO * rows, D), BF16),
            pltpu.VMEM((MICRO, rows, HEADS), F32),
            pltpu.VMEM((MICRO, rows, D), F32),
            pltpu.VMEM((MICRO * rows, D), BF16),
            pltpu.VMEM((MICRO * rows, FF), BF16),
            pltpu.VMEM((MICRO * rows, FF), BF16),
            pltpu.VMEM((MICRO * rows, FF), BF16),
            pltpu.VMEM((MICRO * rows, D), BF16),
            pltpu.VMEM((MICRO * rows, D), BF16),
            pltpu.VMEM((MICRO * rows, D), BF16),
            pltpu.VMEM((MICRO * window, 2 * D), BF16),
            pltpu.VMEM((rows, D), BF16),
            pltpu.VMEM((MICRO, rows, D), F32),
            pltpu.VMEM((MICRO, 2, rows, D), BF16),
            pltpu.VMEM((MICRO, 2, rows, D), BF16),
            pltpu.VMEM((MICRO, rows, D), BF16),
            pltpu.VMEM((MICRO, rows, D), BF16),
            pltpu.VMEM((GRAD_ROWS, D), BF16),
            pltpu.VMEM((GRAD_ROWS, D), BF16),
            pltpu.VMEM((GRAD_ROWS, D), BF16),
            pltpu.VMEM((SMALL_ROWS, D), F32),
            pltpu.VMEM((2, levels, SMALL_ROWS, D), F32),
            dma((12,)),
            dma((2 + 12,)),
            dma((MICRO, 2, CHUNKS)),
            dma((MICRO, 2, CHUNKS)),
            dma((MICRO, 2, CHUNKS)),
            dma((MICRO, 2, CHUNKS)),
            dma((MICRO, CHUNKS)),
            dma((MICRO, CHUNKS)),
            dma((tasks, 2 * levels)),
            dma((tasks, 2 * levels)),
            dma((levels,)),
            dma((levels,)),
        ],
        compiler_params=pltpu.CompilerParams(
            collective_id=1, has_side_effects=True, vmem_limit_bytes=63 * 1024 * 1024
        ),
        name="layers",
    )(
        features,
        cotangent,
        sigma_embed,
        neighbours.T,
        valid_slots.T,
        ada_weight,
        ada_bias,
        qkv_weight,
        out_weight,
        up_weight,
        up_bias,
        down_weight,
        down_bias,
    )
    boundary, grad_qkv, grad_out, grad_up, grad_down, small = outs
    return pl.pallas_call(
        widen_kernel,
        out_shape=(
            jax.ShapeDtypeStruct(boundary.shape, F32),
            jax.ShapeDtypeStruct((1, D, 4 * D), F32),
            jax.ShapeDtypeStruct((1, 4 * D), F32),
            jax.ShapeDtypeStruct((1, D, 3 * D), F32),
            jax.ShapeDtypeStruct((1, D, D), F32),
            jax.ShapeDtypeStruct((1, D, FF), F32),
            jax.ShapeDtypeStruct((1, FF), F32),
            jax.ShapeDtypeStruct((1, FF, D), F32),
            jax.ShapeDtypeStruct((1, D), F32),
        ),
        in_specs=[every] * 5 + [vmem, vmem],
        out_specs=[every, every, vmem, every, every, every, vmem, every, vmem],
        scratch_shapes=[
            pltpu.VMEM((GRAD_ROWS, D), BF16),
            pltpu.VMEM((GRAD_ROWS, D), F32),
            pltpu.VMEM((4 * D, D), F32),
            pltpu.VMEM(boundary.shape, F32),
            dma((13,)),
            dma((17,)),
        ],
        compiler_params=pltpu.CompilerParams(vmem_limit_bytes=60 * 1024 * 1024),
        name="widen",
    )(boundary, grad_qkv, grad_out, grad_up, grad_down, small, sigma_embed)


def widen_kernel(
    boundary,
    grad_qkv,
    grad_out,
    grad_up,
    grad_down,
    small,
    sigma,
    boundary_wide,
    ada_wide,
    ada_bias_wide,
    qkv_wide,
    out_wide,
    up_wide,
    up_bias_wide,
    down_wide,
    down_bias_wide,
    narrow,
    broad,
    outer,
    held,
    load_sem,
    store_sem,
):
    def blocks(down, up, out, qkv):
        return (
            [down.at[pl.ds(j * D, D)] for j in range(4)]
            + [up.at[:, pl.ds(j * D, D)] for j in range(4)]
            + [out]
            + [qkv.at[:, pl.ds(j * D, D)] for j in range(3)]
        )

    rest = pltpu.make_async_copy(boundary, held, load_sem.at[12])
    rest.start()
    loads, stores = [], []
    for i, source in enumerate(blocks(grad_down, grad_up, grad_out, grad_qkv)):
        loads.append(pltpu.make_async_copy(source, narrow.at[pl.ds(i * D, D)], load_sem.at[i]))
        loads[-1].start()
    column = jnp.transpose(sigma[...].astype(F32))
    for j in range(4):
        part = slice(j * D, (j + 1) * D)
        outer[part] = column[:, 0:1] * small[j : j + 1] + column[:, 1:2] * small[4 + j : 5 + j]
        ada_bias_wide[:, part] = small[j : j + 1] + small[4 + j : 5 + j]
        up_bias_wide[:, part] = small[8 + j : 9 + j]
        stores.append(
            pltpu.make_async_copy(
                outer.at[pl.ds(j * D, D)], ada_wide.at[0, :, pl.ds(j * D, D)], store_sem.at[12 + j]
            )
        )
        stores[-1].start()
    down_bias_wide[...] = small[12:13]
    rest.wait()
    stores.append(pltpu.make_async_copy(held, boundary_wide, store_sem.at[16]))
    stores[-1].start()
    targets = blocks(down_wide.at[0], up_wide.at[0], out_wide.at[0], qkv_wide.at[0])
    for i, target in enumerate(targets):
        loads[i].wait()
        part = slice(i * D, (i + 1) * D)
        broad[part] = narrow[part].astype(F32)
        stores.append(pltpu.make_async_copy(broad.at[pl.ds(i * D, D)], target, store_sem.at[i]))
        stores[-1].start()
    for copy in stores:
        copy.wait()


def solution(mesh):
    return jax.shard_map(
        shards,
        mesh=mesh,
        in_specs=(
            P(None, "wide", None),
            P(),
            P(None, "wide", None),
            P("wide", None),
            P("wide", None),
            P("section", None, None),
            P("section", None),
            P("section", None, None),
            P("section", None, None),
            P("section", None, None),
            P("section", None),
            P("section", None, None),
            P("section", None),
        ),
        out_specs=(
            P("section", None, "wide", None),
            P("section", None, None),
            P("section", None),
            P("section", None, None),
            P("section", None, None),
            P("section", None, None),
            P("section", None),
            P("section", None, None),
            P("section", None),
        ),
        check_vma=False,
    )
```

```python
import functools
import math

import jax
import jax.numpy as jnp
from jax import lax
from jax.experimental import pallas as pl
from jax.experimental.pallas import tpu as pltpu
from jax.sharding import PartitionSpec as P

D = 512
FF = 2048
HEADS = 4
HEAD_DIM = 128
NEIGHBOURS = 16
MICRO = 2
GRAD_ROWS = 12 * D
SMALL_ROWS = 16
CHUNKS = 4
ORDER = (
    (2, 0), (1, 0), (0, 0), (2, 1), (3, 0), (1, 1), "gate", (3, 1), (4, 0), (5, 0), (0, 1), (6, 0), (2, 2),
    (4, 1), "dense", (8, 0), (6, 1), (3, 2), (1, 2), "head0", (5, 1), (4, 2), (7, 0), (7, 1), (0, 2), (6, 2),
    (3, 3), (8, 1), (2, 3), "head1", "head2", (5, 2), "head3", (4, 3), "back", (10, 0), (3, 4), (11, 0),
    (8, 2), (11, 1), (5, 3), (0, 3), (7, 2), (2, 4), (4, 4), (9, 0), (9, 1), (3, 5), (1, 3), (5, 4), (6, 3),
    "end0", (2, 5), (8, 3), (7, 3), (10, 1), (4, 5), (11, 2), (9, 2), (6, 4), (5, 5), (2, 6), (4, 6), (8, 4),
    (9, 3), (10, 2), (11, 3), (6, 5), (3, 6), (5, 6), (7, 4), (2, 7), (8, 5), (10, 3), (11, 4), (0, 4),
    (1, 4), (6, 6), (7, 5), (9, 4), (10, 4), (8, 6), (11, 5), "end1", (1, 5), (9, 5), (4, 7), (7, 6), (0, 5),
    (4, 8), (10, 5), (11, 6), (9, 6), (1, 6), (8, 7), (7, 7), (3, 7), (5, 7), (0, 6), (10, 6), (3, 8),
    (8, 8), (6, 7), (6, 8), (11, 7), (1, 7), (9, 7), (9, 8), (5, 8), (0, 7), (11, 8), (2, 8), (10, 7),
    (0, 8), (1, 8), (7, 8), (10, 8),
)

norm_epsilon = 1e-05
masked_score = -1e30
LOG2E = math.log2(math.e)
SCORE_SCALE = HEAD_DIM**-0.5

MESH = pl.DeviceIdType.MESH
BF16 = jnp.bfloat16
F32 = jnp.float32


def mm(left, right):
    return jnp.dot(left, right, preferred_element_type=F32)


def mm_nt(left, right):
    return lax.dot_general(left, right, (((1,), (1,)), ((), ())), preferred_element_type=F32)


def mm_tn(left, right):
    return lax.dot_general(left, right, (((0,), (0,)), ((), ())), preferred_element_type=F32)


def row_mean(values):
    return jnp.mean(values, axis=-1, keepdims=True)


def normalize(values):
    center = values - row_mean(values)
    inverse = lax.rsqrt(row_mean(center * center) + norm_epsilon)
    return center * inverse, inverse


def column_sum(values):
    return jnp.sum(values, axis=0, keepdims=True)


def layer_kernel(
    sections,
    wide,
    features,
    cotangent,
    sigma,
    neighbours,
    valid_slots,
    ada_weight,
    ada_bias,
    qkv_weight,
    out_weight,
    up_weight,
    up_bias,
    down_weight,
    down_bias,
    boundary,
    grad_qkv_out,
    grad_out_out,
    grad_up_out,
    grad_down_out,
    small_out,
    w_qkv,
    w_out,
    w_up,
    w_down,
    mod,
    slots,
    bias,
    x_in,
    g_out,
    near,
    query,
    key_value,
    attended,
    log_sum,
    mixed,
    normed_b,
    active,
    slope,
    grad_low,
    grad_mixed_low,
    grad_query,
    grad_kv,
    grad_attended,
    grad_near,
    sent_near,
    back_near,
    sent_x,
    arrived_x,
    grads,
    landing,
    gathered,
    small,
    small_landing,
    load_sem,
    store_sem,
    halo_send,
    halo_recv,
    back_send,
    back_recv,
    x_send,
    x_recv,
    ring_send,
    ring_recv,
    small_send,
    small_recv,
):
    sec = lax.axis_index("section")
    me = lax.axis_index("wide")
    rows = x_in.shape[1]
    window = 3 * rows
    levels = wide.bit_length() - 1
    left = lax.rem(me + wide - 1, wide)
    right = lax.rem(me + 1, wide)
    first = sec == 0
    second = sec == 1

    def bit_of(level):
        return lax.rem(lax.div(me, 1 << level), 2)

    def partner(level):
        return me + (1 - 2 * bit_of(level)) * (1 << level)

    loads = []

    def load(source, target):
        copy = pltpu.make_async_copy(source, target, load_sem.at[len(loads)])
        loads.append(copy)
        return copy

    feature_loads = [load(features.at[m], x_in.at[m]) for m in range(MICRO)]
    ada_loads = [
        load(ada_weight.at[0, :, pl.ds(j * D, D)], gathered.at[pl.ds(j * D, D)]) for j in range(4)
    ]
    qkv_load = load(qkv_weight.at[0], w_qkv)
    out_load = load(out_weight.at[0], w_out)
    up_load = load(up_weight.at[0], w_up)
    down_load = load(down_weight.at[0], w_down)
    cotangent_loads = [load(cotangent.at[m], g_out.at[m]) for m in range(MICRO)]

    @pl.when(first)
    def _():
        for copy in feature_loads:
            copy.start()

    for copy in ada_loads:
        copy.start()
    for copy in (qkv_load, out_load, up_load, down_load):
        copy.start()

    @pl.when(second)
    def _():
        for copy in cotangent_loads:
            copy.start()

    barrier = pltpu.get_barrier_semaphore()
    peers = [(sec, left), (sec, right), (1 - sec, me)] + [
        (sec, partner(level)) for level in range(levels)
    ]
    for peer in peers:
        pl.semaphore_signal(barrier, inc=1, device_id=peer, device_id_type=MESH)

    def count_slots():
        start = (me - 1) * rows
        total_nodes = rows * wide
        offsets = neighbours[...] - start
        offsets = jnp.where(offsets >= total_nodes, offsets - total_nodes, offsets)
        offsets = jnp.where(offsets < 0, offsets + total_nodes, offsets)
        offsets = jnp.where(valid_slots[...] > 0, offsets, -1)
        slots[...] = jnp.transpose(offsets.astype(F32))
        block = 32

        @pl.loop(0, rows // block)
        def _(step):
            here = pl.ds(pl.multiple_of(step * block, block), block)
            places = slots[here, :].astype(jnp.int32)
            columns = lax.broadcasted_iota(jnp.int32, (block, window), 1)
            counts = jnp.zeros((block, window), F32)
            for slot in range(NEIGHBOURS):
                counts += jnp.where(places[:, slot : slot + 1] == columns, 1.0, 0.0)
            bias[here, :] = jnp.where(
                counts > 0, jnp.log2(jnp.maximum(counts, 1.0)), masked_score
            )

    for j, copy in enumerate(ada_loads):
        copy.wait()
        mod[:, j * D : (j + 1) * D] = (
            mm(sigma[...], gathered[j * D : (j + 1) * D]) + ada_bias[:, j * D : (j + 1) * D]
        )

    pl.semaphore_wait(barrier, len(peers))

    def modulation(m, part):
        return mod[m : m + 1, part * D : (part + 1) * D]

    chunk = rows // CHUNKS

    def halo_copy(m, side, c):
        base = m * window + c * chunk
        return pltpu.make_async_remote_copy(
            src_ref=near.at[pl.ds(base + rows, chunk)],
            dst_ref=near.at[pl.ds(base + 2 * rows * side, chunk)],
            send_sem=halo_send.at[m, side, c],
            recv_sem=halo_recv.at[m, side, c],
            device_id=(sec, left if side else right),
            device_id_type=MESH,
        )

    def back_copy(m, side, c):
        part = pl.ds(c * chunk, chunk)
        return pltpu.make_async_remote_copy(
            src_ref=sent_near.at[m, side, part],
            dst_ref=back_near.at[m, side, part],
            send_sem=back_send.at[m, side, c],
            recv_sem=back_recv.at[m, side, c],
            device_id=(sec, right if side else left),
            device_id_type=MESH,
        )

    def x_copy(m, c):
        part = pl.ds(c * chunk, chunk)
        return pltpu.make_async_remote_copy(
            src_ref=sent_x.at[m, part],
            dst_ref=arrived_x.at[m, part],
            send_sem=x_send.at[m, c],
            recv_sem=x_recv.at[m, c],
            device_id=(1 - sec, me),
            device_id_type=MESH,
        )

    def final_copy(m):
        return pltpu.make_async_copy(grad_near.at[m], boundary.at[0, m], store_sem.at[m])

    def grad_copy(m):
        return pltpu.make_async_copy(mixed.at[m], boundary.at[0, m], store_sem.at[m])

    def start_halo(m, c):
        for side in range(2):
            halo_copy(m, side, c).start()

    def prepare(m, arriving):
        if not arriving:
            feature_loads[m].wait()
        for c in range(CHUNKS):
            part = slice(c * chunk, (c + 1) * chunk)
            if arriving:
                x_copy(m, c).wait_recv()
                x_in[m, part] = arrived_x[m, part].astype(F32)
            unit, _ = normalize(x_in[m, part])
            own = pl.ds(m * window + rows + c * chunk, chunk)
            near[own, :] = (unit * (1.0 + modulation(m, 1)) + modulation(m, 0)).astype(BF16)
            start_halo(m, c)

    def forward(m):
        base = m * window
        own = near[base + rows : base + 2 * rows]
        if m == 0:
            qkv_load.wait()
        query[m] = (mm(own, w_qkv[:, :D]) * (SCORE_SCALE * LOG2E)).astype(BF16)
        key_value[base + rows : base + 2 * rows] = mm(own, w_qkv[:, D:]).astype(BF16)
        for side in range(2):
            for c in range(CHUNKS):
                halo_copy(m, side, c).wait_recv()
        for side in range(2):
            place = base + 2 * rows * side
            key_value[place : place + rows] = mm(near[place : place + rows], w_qkv[:, D:]).astype(
                BF16
            )
        for h in range(HEADS):
            low, high = h * HEAD_DIM, (h + 1) * HEAD_DIM
            scores = mm_nt(query[m, :, low:high], key_value[base : base + window, low:high])
            scores += bias[...]
            top = jnp.max(scores, axis=1, keepdims=True)
            raised = jnp.exp2(scores - top)
            total = jnp.sum(raised, axis=1, keepdims=True)
            part = mm(raised.astype(BF16), key_value[base : base + window, D + low : D + high])
            attended[m * rows : (m + 1) * rows, low:high] = (part / total).astype(BF16)
            log_sum[m, :, h : h + 1] = top + jnp.log2(total)
        mine = slice(m * rows, (m + 1) * rows)
        if m == 0:
            for copy in (out_load, up_load, down_load):
                copy.wait()
        middle = x_in[m] + mm(attended[mine], w_out[...])
        mixed[m] = middle
        unit, _ = normalize(middle)
        normed_b[mine] = (unit * (1.0 + modulation(m, 3)) + modulation(m, 2)).astype(BF16)
        for j in range(FF // D):
            part = slice(j * D, (j + 1) * D)
            hidden = mm(normed_b[mine], w_up[:, part]) + up_bias[:, part]
            gate = 0.5 + 0.5 * jnp.tanh(0.5 * hidden)
            swish = hidden * gate
            active[mine, part] = swish.astype(BF16)
            slope[mine, part] = (gate + swish * (1.0 - gate)).astype(BF16)
        output = mixed[m] + mm(active[mine], w_down[...]) + down_bias[...]

        @pl.when(first)
        def _():
            for c in range(CHUNKS):
                part = slice(c * chunk, (c + 1) * chunk)
                sent_x[m, part] = output[part].astype(BF16)
                x_copy(m, c).start()

        @pl.when(second)
        def _():
            grad_near[m] = output
            final_copy(m).start()

    def take_grad(m):
        mine = slice(m * rows, (m + 1) * rows)

        @pl.when(first)
        def _():
            for c in range(CHUNKS):
                x_copy(m, c).wait_recv()
            g_out[m] = arrived_x[m].astype(F32)

        @pl.when(second)
        def _():
            cotangent_loads[m].wait()

        grad_out = g_out[m]
        grad_low[mine] = grad_out.astype(BF16)
        down_sum = column_sum(grad_out)
        small[12:13] = down_sum if m == 0 else small[12:13] + down_sum

    def backward_gate(m):
        mine = slice(m * rows, (m + 1) * rows)
        for j in range(FF // D):
            part = slice(j * D, (j + 1) * D)
            hidden = mm_nt(grad_low[mine], w_down[part]) * slope[mine, part].astype(F32)
            hidden = hidden.astype(BF16)
            slope[mine, part] = hidden
            up_sum = column_sum(hidden.astype(F32))
            small[8 + j : 9 + j] = up_sum if m == 0 else small[8 + j : 9 + j] + up_sum

    def backward_dense(m):
        mine = slice(m * rows, (m + 1) * rows)
        grad_normed = mm_nt(slope[mine], w_up[...])
        unit, inverse = normalize(mixed[m])
        small[4 * m + 2 : 4 * m + 3] = column_sum(grad_normed)
        small[4 * m + 3 : 4 * m + 4] = column_sum(grad_normed * unit)
        scaled = grad_normed * (1.0 + modulation(m, 3))
        grad_mixed = g_out[m] + inverse * (
            scaled - row_mean(scaled) - unit * row_mean(scaled * unit)
        )
        mixed[m] = grad_mixed
        grad_mixed_low[mine] = grad_mixed.astype(BF16)
        grad_attended[...] = mm_nt(grad_mixed_low[mine], w_out[...]).astype(BF16)

    def backward_heads(m, heads):
        base = m * window
        mine = slice(m * rows, (m + 1) * rows)
        for h in heads:
            low, high = h * HEAD_DIM, (h + 1) * HEAD_DIM
            queries = query[m, :, low:high]
            keys = key_value[base : base + window, low:high]
            values = key_value[base : base + window, D + low : D + high]
            grad = grad_attended[:, low:high]
            inner = jnp.sum(
                grad.astype(F32) * attended[mine, low:high].astype(F32), axis=1, keepdims=True
            )
            soft = jnp.exp2(mm_nt(queries, keys) + bias[...] - log_sum[m, :, h : h + 1])
            grad_soft = mm_nt(grad, values)
            grad_scores = (soft * (grad_soft - inner)).astype(BF16)
            grad_query[mine, low:high] = (mm(grad_scores, keys) * SCORE_SCALE).astype(BF16)
            grad_kv[base : base + window, low:high] = (
                mm_tn(grad_scores, queries) * (1.0 / LOG2E)
            ).astype(BF16)
            grad_kv[base : base + window, D + low : D + high] = mm_tn(
                soft.astype(BF16), grad
            ).astype(BF16)

    def send_back(m):
        base = m * window
        for side in range(2):
            place = base + 2 * rows * side
            sent_near[m, side] = mm_nt(grad_kv[place : place + rows], w_qkv[:, D:]).astype(BF16)
        for c in range(CHUNKS):
            for side in range(2):
                back_copy(m, side, c).start()

    def near_grad(m):
        base = m * window
        mine = slice(m * rows, (m + 1) * rows)

        @pl.when(second)
        def _():
            final_copy(m).wait()

        grad_near[m] = mm_nt(grad_query[mine], w_qkv[:, :D]) + mm_nt(
            grad_kv[base + rows : base + 2 * rows], w_qkv[:, D:]
        )

    def finish(m, returning, chunks=range(CHUNKS)):
        shift_sum = jnp.zeros((1, D), F32) if chunks[0] == 0 else small[4 * m : 4 * m + 1]
        scale_sum = jnp.zeros((1, D), F32) if chunks[0] == 0 else small[4 * m + 1 : 4 * m + 2]
        for c in chunks:
            part = slice(c * chunk, (c + 1) * chunk)
            for side in range(2):
                back_copy(m, side, c).wait_recv()
            grad_normed = (
                grad_near[m, part]
                + back_near[m, 0, part].astype(F32)
                + back_near[m, 1, part].astype(F32)
            )
            unit, inverse = normalize(x_in[m, part])
            scaled = grad_normed * (1.0 + modulation(m, 1))
            grad_in = mixed[m, part] + inverse * (
                scaled - row_mean(scaled) - unit * row_mean(scaled * unit)
            )
            if returning:
                sent_x[m, part] = grad_in.astype(BF16)
                x_copy(m, c).start()
            else:
                mixed[m, part] = grad_in
            shift_sum += column_sum(grad_normed)
            scale_sum += column_sum(grad_normed * unit)
        small[4 * m : 4 * m + 1] = shift_sum
        small[4 * m + 1 : 4 * m + 2] = scale_sum
        if not returning:
            grad_copy(m).start()

    def weight_grad(block):
        if block < 4:
            value = mm_tn(active[:, block * D : (block + 1) * D], grad_low[...])
        elif block < 8:
            value = mm_tn(normed_b[...], slope[:, (block - 4) * D : (block - 3) * D])
        elif block == 8:
            value = mm_tn(attended[...], grad_mixed_low[...])
        elif block == 9:
            value = sum(
                mm_tn(
                    near[m * window + rows : m * window + 2 * rows],
                    grad_query[m * rows : (m + 1) * rows],
                )
                for m in range(MICRO)
            )
        else:
            value = mm_tn(near[...], grad_kv[:, (block - 10) * D : (block - 9) * D])
        grads[block * D : (block + 1) * D] = value.astype(BF16)

    def block_target(block):
        if block < 4:
            return grad_down_out.at[pl.ds(block * D, D)]
        if block < 8:
            return grad_up_out.at[:, pl.ds((block - 4) * D, D)]
        if block == 8:
            return grad_out_out
        return grad_qkv_out.at[:, pl.ds((block - 9) * D, D)]

    task_rows = max(D, 16 * wide)
    tasks = GRAD_ROWS // task_rows
    per_task = task_rows // D

    def order(task):
        if task < 2 and levels > 2:
            return [0] + list(range(2, levels)) + [1]
        return list(range(levels))

    def segment(task, stage):
        base = task * task_rows
        size = task_rows
        for level in order(task)[:stage]:
            size //= 2
            base = base + bit_of(level) * size
        return base, size

    def halving(task, stage):
        level = order(task)[stage]
        base, size = segment(task, stage)
        half = size // 2
        away = pl.multiple_of(base + (1 - bit_of(level)) * half, 16)
        spot = task * task_rows + task_rows - size
        return pltpu.make_async_remote_copy(
            src_ref=grads.at[pl.ds(away, half)],
            dst_ref=landing.at[pl.ds(spot, half)],
            send_sem=ring_send.at[task, stage],
            recv_sem=ring_recv.at[task, stage],
            device_id=(sec, partner(level)),
            device_id_type=MESH,
        )

    def doubling(task, stage):
        level = order(task)[levels - 1 - stage]
        base, size = segment(task, levels - stage)
        place = pl.ds(pl.multiple_of(base, 16), size)
        return pltpu.make_async_remote_copy(
            src_ref=gathered.at[place],
            dst_ref=gathered.at[place],
            send_sem=ring_send.at[task, levels + stage],
            recv_sem=ring_recv.at[task, levels + stage],
            device_id=(sec, partner(level)),
            device_id_type=MESH,
        )

    def reduce_step(task, stage):
        if stage == 0:
            halving(task, 0).start()
            return
        if stage <= levels:
            halving(task, stage - 1).wait_recv()
            base, size = segment(task, stage)
            spot = task * task_rows + task_rows - 2 * size
            place = pl.ds(pl.multiple_of(base, 16), size)
            value = grads[place, :].astype(F32) + landing[spot : spot + size].astype(F32)
            if stage < levels:
                grads[place, :] = value.astype(BF16)
                halving(task, stage).start()
            else:
                gathered[place, :] = value.astype(BF16)
                doubling(task, 0).start()
            return
        doubling(task, stage - levels - 1).wait_recv()
        if stage < 2 * levels:
            doubling(task, stage - levels).start()
        else:
            for block in range(task * per_task, (task + 1) * per_task):
                pltpu.make_async_copy(
                    gathered.at[pl.ds(block * D, D)], block_target(block), store_sem.at[2 + block]
                ).start()

    def small_copy(level):
        return pltpu.make_async_remote_copy(
            src_ref=small.at[pl.ds(0, SMALL_ROWS)] if level == 0 else small_landing.at[1, level],
            dst_ref=small_landing.at[0, level],
            send_sem=small_send.at[level],
            recv_sem=small_recv.at[level],
            device_id=(sec, partner(level)),
            device_id_type=MESH,
        )

    def small_step(level):
        if level > 0:
            small_copy(level - 1).wait_recv()
            held = small[...] if level == 1 else small_landing[1, level - 1]
            value = held + small_landing[0, level - 1]
            if level == levels:
                small_landing[1, 0] = value
                return
            small_landing[1, level] = value
        small_copy(level).start()

    small[13:SMALL_ROWS] = jnp.zeros((SMALL_ROWS - 13, D), F32)

    @pl.when(first)
    def _():
        prepare(0, False)
        prepare(1, False)

    count_slots()

    @pl.when(second)
    def _():
        prepare(0, True)
        prepare(1, True)

    for m in range(MICRO):
        forward(m)

    @pl.when(first)
    def _():
        for m in range(MICRO):
            for c in range(CHUNKS):
                x_copy(m, c).wait_send()

    take_grad(0)
    backward_gate(0)
    backward_dense(0)
    backward_heads(0, range(HEADS))
    send_back(0)

    @pl.when(first)
    def _():
        near_grad(0)

    take_grad(1)

    @pl.when(second)
    def _():
        backward_gate(1)
        backward_dense(1)
        backward_heads(1, range(3))
        near_grad(0)
        finish(0, True, range(2))
        backward_heads(1, range(3, HEADS))
        finish(0, True, range(2, CHUNKS))
        send_back(1)
        near_grad(1)
        finish(1, True)

    def end(m):
        if m == 1:
            near_grad(1)
        finish(m, False)

    extras = {"gate": functools.partial(backward_gate, 1)}
    extras["dense"] = functools.partial(backward_dense, 1)
    for h in range(HEADS):
        extras[f"head{h}"] = functools.partial(backward_heads, 1, [h])
    extras["back"] = functools.partial(send_back, 1)
    extras["end0"] = functools.partial(end, 0)
    extras["end1"] = functools.partial(end, 1)

    if levels == 4 and tasks == 12:
        plan = ORDER
    else:
        plan = list(extras)
        for moment in range(tasks + 4 * levels):
            for stage in range(2 * levels, -1, -1):
                if 0 <= moment - 2 * stage < tasks:
                    plan.append((moment - 2 * stage, stage))
    ended = False
    level = 0
    for item in plan:
        if item in extras:
            pl.when(first)(extras[item])
            ended = ended or item == "end1"
            continue
        task, stage = item
        if stage == 0:
            for block in range(task * per_task, (task + 1) * per_task):
                weight_grad(block)
        reduce_step(task, stage)
        if ended and level <= levels and stage >= 2:
            small_step(level)
            level += 1
    for level in range(level, levels + 1):
        small_step(level)
    small_out[...] = small_landing[1, 0]

    for m in range(MICRO):
        for side in range(2):
            for c in range(CHUNKS):
                halo_copy(m, side, c).wait_send()
                back_copy(m, side, c).wait_send()

    @pl.when(first)
    def _():
        for m in range(MICRO):
            grad_copy(m).wait()

    @pl.when(second)
    def _():
        for m in range(MICRO):
            for c in range(CHUNKS):
                x_copy(m, c).wait_send()

    for task in range(tasks):
        for stage in range(levels):
            halving(task, stage).wait_send()
            doubling(task, stage).wait_send()
    for level in range(levels):
        small_copy(level).wait_send()
    for block in range(12):
        pltpu.make_async_copy(
            gathered.at[pl.ds(block * D, D)], block_target(block), store_sem.at[2 + block]
        ).wait()


def shards(
    features,
    sigma_embed,
    cotangent,
    neighbours,
    valid_slots,
    ada_weight,
    ada_bias,
    qkv_weight,
    out_weight,
    up_weight,
    up_bias,
    down_weight,
    down_bias,
):
    rows = features.shape[1]
    wide = lax.axis_size("wide")
    sections = lax.axis_size("section")
    levels = wide.bit_length() - 1
    tasks = GRAD_ROWS // max(D, 16 * wide)
    window = 3 * rows
    every = pl.BlockSpec(memory_space=pl.ANY)
    vmem = pl.BlockSpec(memory_space=pltpu.VMEM)
    dma = pltpu.SemaphoreType.DMA
    outs = pl.pallas_call(
        functools.partial(layer_kernel, sections, wide),
        out_shape=(
            jax.ShapeDtypeStruct((1, MICRO, rows, D), F32),
            jax.ShapeDtypeStruct((D, 3 * D), BF16),
            jax.ShapeDtypeStruct((D, D), BF16),
            jax.ShapeDtypeStruct((D, FF), BF16),
            jax.ShapeDtypeStruct((FF, D), BF16),
            jax.ShapeDtypeStruct((SMALL_ROWS, D), F32),
        ),
        in_specs=[every, every, vmem, vmem, vmem, every, vmem, every, every, every, vmem, every, vmem],
        out_specs=[every, every, every, every, every, vmem],
        scratch_shapes=[
            pltpu.VMEM((D, 3 * D), BF16),
            pltpu.VMEM((D, D), BF16),
            pltpu.VMEM((D, FF), BF16),
            pltpu.VMEM((FF, D), BF16),
            pltpu.VMEM((MICRO, 4 * D), F32),
            pltpu.VMEM((rows, NEIGHBOURS), F32),
            pltpu.VMEM((rows, window), F32),
            pltpu.VMEM((MICRO, rows, D), F32),
            pltpu.VMEM((MICRO, rows, D), F32),
            pltpu.VMEM((MICRO * window, D), BF16),
            pltpu.VMEM((MICRO, rows, D), BF16),
            pltpu.VMEM((MICRO * window, 2 * D), BF16),
            pltpu.VMEM((MICRO * rows, D), BF16),
            pltpu.VMEM((MICRO, rows, HEADS), F32),
            pltpu.VMEM((MICRO, rows, D), F32),
            pltpu.VMEM((MICRO * rows, D), BF16),
            pltpu.VMEM((MICRO * rows, FF), BF16),
            pltpu.VMEM((MICRO * rows, FF), BF16),
            pltpu.VMEM((MICRO * rows, D), BF16),
            pltpu.VMEM((MICRO * rows, D), BF16),
            pltpu.VMEM((MICRO * rows, D), BF16),
            pltpu.VMEM((MICRO * window, 2 * D), BF16),
            pltpu.VMEM((rows, D), BF16),
            pltpu.VMEM((MICRO, rows, D), F32),
            pltpu.VMEM((MICRO, 2, rows, D), BF16),
            pltpu.VMEM((MICRO, 2, rows, D), BF16),
            pltpu.VMEM((MICRO, rows, D), BF16),
            pltpu.VMEM((MICRO, rows, D), BF16),
            pltpu.VMEM((GRAD_ROWS, D), BF16),
            pltpu.VMEM((GRAD_ROWS, D), BF16),
            pltpu.VMEM((GRAD_ROWS, D), BF16),
            pltpu.VMEM((SMALL_ROWS, D), F32),
            pltpu.VMEM((2, levels, SMALL_ROWS, D), F32),
            dma((12,)),
            dma((2 + 12,)),
            dma((MICRO, 2, CHUNKS)),
            dma((MICRO, 2, CHUNKS)),
            dma((MICRO, 2, CHUNKS)),
            dma((MICRO, 2, CHUNKS)),
            dma((MICRO, CHUNKS)),
            dma((MICRO, CHUNKS)),
            dma((tasks, 2 * levels)),
            dma((tasks, 2 * levels)),
            dma((levels,)),
            dma((levels,)),
        ],
        compiler_params=pltpu.CompilerParams(
            collective_id=1, has_side_effects=True, vmem_limit_bytes=63 * 1024 * 1024
        ),
        name="layers",
    )(
        features,
        cotangent,
        sigma_embed,
        neighbours.T,
        valid_slots.T,
        ada_weight,
        ada_bias,
        qkv_weight,
        out_weight,
        up_weight,
        up_bias,
        down_weight,
        down_bias,
    )
    boundary, grad_qkv, grad_out, grad_up, grad_down, small = outs
    return pl.pallas_call(
        widen_kernel,
        out_shape=(
            jax.ShapeDtypeStruct(boundary.shape, F32),
            jax.ShapeDtypeStruct((1, D, 4 * D), F32),
            jax.ShapeDtypeStruct((1, 4 * D), F32),
            jax.ShapeDtypeStruct((1, D, 3 * D), F32),
            jax.ShapeDtypeStruct((1, D, D), F32),
            jax.ShapeDtypeStruct((1, D, FF), F32),
            jax.ShapeDtypeStruct((1, FF), F32),
            jax.ShapeDtypeStruct((1, FF, D), F32),
            jax.ShapeDtypeStruct((1, D), F32),
        ),
        in_specs=[every] * 5 + [vmem, vmem],
        out_specs=[every, every, vmem, every, every, every, vmem, every, vmem],
        scratch_shapes=[
            pltpu.VMEM((GRAD_ROWS, D), BF16),
            pltpu.VMEM((GRAD_ROWS, D), F32),
            pltpu.VMEM((4 * D, D), F32),
            pltpu.VMEM(boundary.shape, F32),
            dma((13,)),
            dma((17,)),
        ],
        compiler_params=pltpu.CompilerParams(vmem_limit_bytes=60 * 1024 * 1024),
        name="widen",
    )(boundary, grad_qkv, grad_out, grad_up, grad_down, small, sigma_embed)


def widen_kernel(
    boundary,
    grad_qkv,
    grad_out,
    grad_up,
    grad_down,
    small,
    sigma,
    boundary_wide,
    ada_wide,
    ada_bias_wide,
    qkv_wide,
    out_wide,
    up_wide,
    up_bias_wide,
    down_wide,
    down_bias_wide,
    narrow,
    broad,
    outer,
    held,
    load_sem,
    store_sem,
):
    def blocks(down, up, out, qkv):
        return (
            [down.at[pl.ds(j * D, D)] for j in range(4)]
            + [up.at[:, pl.ds(j * D, D)] for j in range(4)]
            + [out]
            + [qkv.at[:, pl.ds(j * D, D)] for j in range(3)]
        )

    rest = pltpu.make_async_copy(boundary, held, load_sem.at[12])
    rest.start()
    loads, stores = [], []
    for i, source in enumerate(blocks(grad_down, grad_up, grad_out, grad_qkv)):
        loads.append(pltpu.make_async_copy(source, narrow.at[pl.ds(i * D, D)], load_sem.at[i]))
        loads[-1].start()
    column = jnp.transpose(sigma[...].astype(F32))
    for j in range(4):
        part = slice(j * D, (j + 1) * D)
        outer[part] = column[:, 0:1] * small[j : j + 1] + column[:, 1:2] * small[4 + j : 5 + j]
        ada_bias_wide[:, part] = small[j : j + 1] + small[4 + j : 5 + j]
        up_bias_wide[:, part] = small[8 + j : 9 + j]
        stores.append(
            pltpu.make_async_copy(
                outer.at[pl.ds(j * D, D)], ada_wide.at[0, :, pl.ds(j * D, D)], store_sem.at[12 + j]
            )
        )
        stores[-1].start()
    down_bias_wide[...] = small[12:13]
    rest.wait()
    stores.append(pltpu.make_async_copy(held, boundary_wide, store_sem.at[16]))
    stores[-1].start()
    targets = blocks(down_wide.at[0], up_wide.at[0], out_wide.at[0], qkv_wide.at[0])
    for i, target in enumerate(targets):
        loads[i].wait()
        part = slice(i * D, (i + 1) * D)
        broad[part] = narrow[part].astype(F32)
        stores.append(pltpu.make_async_copy(broad.at[pl.ds(i * D, D)], target, store_sem.at[i]))
        stores[-1].start()
    for copy in stores:
        copy.wait()


def solution(mesh):
    return jax.shard_map(
        shards,
        mesh=mesh,
        in_specs=(
            P(None, "wide", None),
            P(),
            P(None, "wide", None),
            P("wide", None),
            P("wide", None),
            P("section", None, None),
            P("section", None),
            P("section", None, None),
            P("section", None, None),
            P("section", None, None),
            P("section", None),
            P("section", None, None),
            P("section", None),
        ),
        out_specs=(
            P("section", None, "wide", None),
            P("section", None, None),
            P("section", None),
            P("section", None, None),
            P("section", None, None),
            P("section", None, None),
            P("section", None),
            P("section", None, None),
            P("section", None),
        ),
        check_vma=False,
    )
```

```python
import functools
import math

import jax
import jax.numpy as jnp
from jax import lax
from jax.experimental import pallas as pl
from jax.experimental.pallas import tpu as pltpu
from jax.sharding import PartitionSpec as P

D = 512
FF = 2048
HEADS = 4
HEAD_DIM = 128
NEIGHBOURS = 16
MICRO = 2
GRAD_ROWS = 12 * D
SMALL_ROWS = 16
CHUNKS = 4
ORDER = (
    (2, 0), (1, 0), (0, 0), (2, 1), (3, 0), (1, 1), "gate", (3, 1), (4, 0), (5, 0), (0, 1), (6, 0), (2, 2),
    (4, 1), "dense", (8, 0), (6, 1), (3, 2), (1, 2), "head0", (5, 1), (4, 2), (7, 0), (7, 1), (0, 2), (6, 2),
    (3, 3), (8, 1), (2, 3), "head1", "head2", (5, 2), "head3", (4, 3), "back", (10, 0), (3, 4), (11, 0),
    (8, 2), (11, 1), (5, 3), (0, 3), (7, 2), (2, 4), (4, 4), (9, 0), (9, 1), (3, 5), (1, 3), (5, 4), (6, 3),
    "end0", (2, 5), (8, 3), (7, 3), (10, 1), (4, 5), (11, 2), (9, 2), (6, 4), (5, 5), (2, 6), (4, 6), (8, 4),
    (9, 3), (10, 2), (11, 3), (6, 5), (3, 6), (5, 6), (7, 4), (2, 7), (8, 5), (10, 3), (11, 4), (0, 4),
    (1, 4), (6, 6), (7, 5), (9, 4), (10, 4), (8, 6), (11, 5), "end1", (1, 5), (9, 5), (4, 7), (7, 6), (0, 5),
    (4, 8), (10, 5), (11, 6), (9, 6), (1, 6), (8, 7), (7, 7), (3, 7), (5, 7), (0, 6), (10, 6), (3, 8),
    (8, 8), (6, 7), (6, 8), (11, 7), (1, 7), (9, 7), (9, 8), (5, 8), (0, 7), (11, 8), (2, 8), (10, 7),
    (0, 8), (1, 8), (7, 8), (10, 8),
)

norm_epsilon = 1e-05
masked_score = -1e30
LOG2E = math.log2(math.e)
SCORE_SCALE = HEAD_DIM**-0.5

MESH = pl.DeviceIdType.MESH
BF16 = jnp.bfloat16
F32 = jnp.float32


def mm(left, right):
    return jnp.dot(left, right, preferred_element_type=F32)


def mm_nt(left, right):
    return lax.dot_general(left, right, (((1,), (1,)), ((), ())), preferred_element_type=F32)


def mm_tn(left, right):
    return lax.dot_general(left, right, (((0,), (0,)), ((), ())), preferred_element_type=F32)


def row_mean(values):
    return jnp.mean(values, axis=-1, keepdims=True)


def normalize(values):
    center = values - row_mean(values)
    inverse = lax.rsqrt(row_mean(center * center) + norm_epsilon)
    return center * inverse, inverse


def column_sum(values):
    return jnp.sum(values, axis=0, keepdims=True)


def layer_kernel(
    sections,
    wide,
    features,
    cotangent,
    sigma,
    neighbours,
    valid_slots,
    ada_weight,
    ada_bias,
    qkv_weight,
    out_weight,
    up_weight,
    up_bias,
    down_weight,
    down_bias,
    boundary,
    grad_qkv_out,
    grad_out_out,
    grad_up_out,
    grad_down_out,
    small_out,
    w_qkv,
    w_out,
    w_up,
    w_down,
    mod,
    slots,
    bias,
    x_in,
    g_out,
    near,
    query,
    key_value,
    attended,
    log_sum,
    mixed,
    normed_b,
    active,
    slope,
    grad_low,
    grad_mixed_low,
    grad_query,
    grad_kv,
    grad_attended,
    grad_near,
    sent_near,
    back_near,
    sent_x,
    arrived_x,
    grads,
    landing,
    gathered,
    small,
    small_landing,
    load_sem,
    store_sem,
    halo_send,
    halo_recv,
    back_send,
    back_recv,
    x_send,
    x_recv,
    ring_send,
    ring_recv,
    small_send,
    small_recv,
):
    sec = lax.axis_index("section")
    me = lax.axis_index("wide")
    rows = x_in.shape[1]
    window = 3 * rows
    levels = wide.bit_length() - 1
    left = lax.rem(me + wide - 1, wide)
    right = lax.rem(me + 1, wide)
    first = sec == 0
    second = sec == 1

    def bit_of(level):
        return lax.rem(lax.div(me, 1 << level), 2)

    def partner(level):
        return me + (1 - 2 * bit_of(level)) * (1 << level)

    loads = []

    def load(source, target):
        copy = pltpu.make_async_copy(source, target, load_sem.at[len(loads)])
        loads.append(copy)
        return copy

    feature_loads = [load(features.at[m], x_in.at[m]) for m in range(MICRO)]
    ada_loads = [
        load(ada_weight.at[0, :, pl.ds(j * D, D)], gathered.at[pl.ds(j * D, D)]) for j in range(4)
    ]
    qkv_load = load(qkv_weight.at[0], w_qkv)
    out_load = load(out_weight.at[0], w_out)
    up_load = load(up_weight.at[0], w_up)
    down_load = load(down_weight.at[0], w_down)
    cotangent_loads = [load(cotangent.at[m], g_out.at[m]) for m in range(MICRO)]

    @pl.when(first)
    def _():
        for copy in feature_loads:
            copy.start()

    for copy in ada_loads:
        copy.start()
    for copy in (qkv_load, out_load, up_load, down_load):
        copy.start()

    @pl.when(second)
    def _():
        for copy in cotangent_loads:
            copy.start()

    barrier = pltpu.get_barrier_semaphore()
    peers = [(sec, left), (sec, right), (1 - sec, me)] + [
        (sec, partner(level)) for level in range(levels)
    ]
    for peer in peers:
        pl.semaphore_signal(barrier, inc=1, device_id=peer, device_id_type=MESH)

    def count_slots():
        start = (me - 1) * rows
        total_nodes = rows * wide
        offsets = neighbours[...] - start
        offsets = jnp.where(offsets >= total_nodes, offsets - total_nodes, offsets)
        offsets = jnp.where(offsets < 0, offsets + total_nodes, offsets)
        offsets = jnp.where(valid_slots[...] > 0, offsets, -1)
        slots[...] = jnp.transpose(offsets.astype(F32))
        block = 32

        @pl.loop(0, rows // block)
        def _(step):
            here = pl.ds(pl.multiple_of(step * block, block), block)
            places = slots[here, :].astype(jnp.int32)
            columns = lax.broadcasted_iota(jnp.int32, (block, window), 1)
            counts = jnp.zeros((block, window), F32)
            for slot in range(NEIGHBOURS):
                counts += jnp.where(places[:, slot : slot + 1] == columns, 1.0, 0.0)
            bias[here, :] = jnp.where(
                counts > 0, jnp.log2(jnp.maximum(counts, 1.0)), masked_score
            )

    def make_modulation(parts):
        for j in parts:
            ada_loads[j].wait()
            mod[:, j * D : (j + 1) * D] = (
                mm(sigma[...], gathered[j * D : (j + 1) * D]) + ada_bias[:, j * D : (j + 1) * D]
            )

    make_modulation((0, 1))
    pl.semaphore_wait(barrier, len(peers))

    def modulation(m, part):
        return mod[m : m + 1, part * D : (part + 1) * D]

    chunk = rows // CHUNKS

    def halo_copy(m, side, c):
        base = m * window + c * chunk
        return pltpu.make_async_remote_copy(
            src_ref=near.at[pl.ds(base + rows, chunk)],
            dst_ref=near.at[pl.ds(base + 2 * rows * side, chunk)],
            send_sem=halo_send.at[m, side, c],
            recv_sem=halo_recv.at[m, side, c],
            device_id=(sec, left if side else right),
            device_id_type=MESH,
        )

    def back_copy(m, side, c):
        part = pl.ds(c * chunk, chunk)
        return pltpu.make_async_remote_copy(
            src_ref=sent_near.at[m, side, part],
            dst_ref=back_near.at[m, side, part],
            send_sem=back_send.at[m, side, c],
            recv_sem=back_recv.at[m, side, c],
            device_id=(sec, right if side else left),
            device_id_type=MESH,
        )

    def x_copy(m, c):
        part = pl.ds(c * chunk, chunk)
        return pltpu.make_async_remote_copy(
            src_ref=sent_x.at[m, part],
            dst_ref=arrived_x.at[m, part],
            send_sem=x_send.at[m, c],
            recv_sem=x_recv.at[m, c],
            device_id=(1 - sec, me),
            device_id_type=MESH,
        )

    def final_copy(m):
        return pltpu.make_async_copy(grad_near.at[m], boundary.at[0, m], store_sem.at[m])

    def grad_copy(m):
        return pltpu.make_async_copy(mixed.at[m], boundary.at[0, m], store_sem.at[m])

    def start_halo(m, c):
        for side in range(2):
            halo_copy(m, side, c).start()

    def prepare(m, arriving):
        if not arriving:
            feature_loads[m].wait()
        for c in range(CHUNKS):
            part = slice(c * chunk, (c + 1) * chunk)
            if arriving:
                x_copy(m, c).wait_recv()
                x_in[m, part] = arrived_x[m, part].astype(F32)
            unit, _ = normalize(x_in[m, part])
            own = pl.ds(m * window + rows + c * chunk, chunk)
            near[own, :] = (unit * (1.0 + modulation(m, 1)) + modulation(m, 0)).astype(BF16)
            start_halo(m, c)

    def forward(m):
        base = m * window
        own = near[base + rows : base + 2 * rows]
        if m == 0:
            qkv_load.wait()
        query[m] = (mm(own, w_qkv[:, :D]) * (SCORE_SCALE * LOG2E)).astype(BF16)
        key_value[base + rows : base + 2 * rows] = mm(own, w_qkv[:, D:]).astype(BF16)
        for side in range(2):
            for c in range(CHUNKS):
                halo_copy(m, side, c).wait_recv()
        for side in range(2):
            place = base + 2 * rows * side
            key_value[place : place + rows] = mm(near[place : place + rows], w_qkv[:, D:]).astype(
                BF16
            )
        for h in range(HEADS):
            low, high = h * HEAD_DIM, (h + 1) * HEAD_DIM
            scores = mm_nt(query[m, :, low:high], key_value[base : base + window, low:high])
            scores += bias[...]
            top = jnp.max(scores, axis=1, keepdims=True)
            raised = jnp.exp2(scores - top)
            total = jnp.sum(raised, axis=1, keepdims=True)
            part = mm(raised.astype(BF16), key_value[base : base + window, D + low : D + high])
            attended[m * rows : (m + 1) * rows, low:high] = (part / total).astype(BF16)
            log_sum[m, :, h : h + 1] = top + jnp.log2(total)
        mine = slice(m * rows, (m + 1) * rows)
        if m == 0:
            for copy in (out_load, up_load, down_load):
                copy.wait()
        middle = x_in[m] + mm(attended[mine], w_out[...])
        mixed[m] = middle
        unit, _ = normalize(middle)
        normed_b[mine] = (unit * (1.0 + modulation(m, 3)) + modulation(m, 2)).astype(BF16)
        for j in range(FF // D):
            part = slice(j * D, (j + 1) * D)
            hidden = mm(normed_b[mine], w_up[:, part]) + up_bias[:, part]
            gate = 0.5 + 0.5 * jnp.tanh(0.5 * hidden)
            swish = hidden * gate
            active[mine, part] = swish.astype(BF16)
            slope[mine, part] = (gate + swish * (1.0 - gate)).astype(BF16)
        output = mixed[m] + mm(active[mine], w_down[...]) + down_bias[...]

        @pl.when(first)
        def _():
            for c in range(CHUNKS):
                part = slice(c * chunk, (c + 1) * chunk)
                sent_x[m, part] = output[part].astype(BF16)
                x_copy(m, c).start()

        @pl.when(second)
        def _():
            grad_near[m] = output
            final_copy(m).start()

    def take_grad(m):
        mine = slice(m * rows, (m + 1) * rows)

        @pl.when(first)
        def _():
            for c in range(CHUNKS):
                x_copy(m, c).wait_recv()
            g_out[m] = arrived_x[m].astype(F32)

        @pl.when(second)
        def _():
            cotangent_loads[m].wait()

        grad_out = g_out[m]
        grad_low[mine] = grad_out.astype(BF16)
        down_sum = column_sum(grad_out)
        small[12:13] = down_sum if m == 0 else small[12:13] + down_sum

    def backward_gate(m):
        mine = slice(m * rows, (m + 1) * rows)
        for j in range(FF // D):
            part = slice(j * D, (j + 1) * D)
            hidden = mm_nt(grad_low[mine], w_down[part]) * slope[mine, part].astype(F32)
            hidden = hidden.astype(BF16)
            slope[mine, part] = hidden
            up_sum = column_sum(hidden.astype(F32))
            small[8 + j : 9 + j] = up_sum if m == 0 else small[8 + j : 9 + j] + up_sum

    def backward_dense(m):
        mine = slice(m * rows, (m + 1) * rows)
        grad_normed = mm_nt(slope[mine], w_up[...])
        unit, inverse = normalize(mixed[m])
        small[4 * m + 2 : 4 * m + 3] = column_sum(grad_normed)
        small[4 * m + 3 : 4 * m + 4] = column_sum(grad_normed * unit)
        scaled = grad_normed * (1.0 + modulation(m, 3))
        grad_mixed = g_out[m] + inverse * (
            scaled - row_mean(scaled) - unit * row_mean(scaled * unit)
        )
        mixed[m] = grad_mixed
        grad_mixed_low[mine] = grad_mixed.astype(BF16)
        grad_attended[...] = mm_nt(grad_mixed_low[mine], w_out[...]).astype(BF16)

    def backward_heads(m, heads):
        base = m * window
        mine = slice(m * rows, (m + 1) * rows)
        for h in heads:
            low, high = h * HEAD_DIM, (h + 1) * HEAD_DIM
            queries = query[m, :, low:high]
            keys = key_value[base : base + window, low:high]
            values = key_value[base : base + window, D + low : D + high]
            grad = grad_attended[:, low:high]
            inner = jnp.sum(
                grad.astype(F32) * attended[mine, low:high].astype(F32), axis=1, keepdims=True
            )
            soft = jnp.exp2(mm_nt(queries, keys) + bias[...] - log_sum[m, :, h : h + 1])
            grad_soft = mm_nt(grad, values)
            grad_scores = (soft * (grad_soft - inner)).astype(BF16)
            grad_query[mine, low:high] = (mm(grad_scores, keys) * SCORE_SCALE).astype(BF16)
            grad_kv[base : base + window, low:high] = (
                mm_tn(grad_scores, queries) * (1.0 / LOG2E)
            ).astype(BF16)
            grad_kv[base : base + window, D + low : D + high] = mm_tn(
                soft.astype(BF16), grad
            ).astype(BF16)

    def send_back(m):
        base = m * window
        for side in range(2):
            place = base + 2 * rows * side
            sent_near[m, side] = mm_nt(grad_kv[place : place + rows], w_qkv[:, D:]).astype(BF16)
        for c in range(CHUNKS):
            for side in range(2):
                back_copy(m, side, c).start()

    def near_grad(m):
        base = m * window
        mine = slice(m * rows, (m + 1) * rows)

        @pl.when(second)
        def _():
            final_copy(m).wait()

        grad_near[m] = mm_nt(grad_query[mine], w_qkv[:, :D]) + mm_nt(
            grad_kv[base + rows : base + 2 * rows], w_qkv[:, D:]
        )

    def finish(m, returning, chunks=range(CHUNKS)):
        shift_sum = jnp.zeros((1, D), F32) if chunks[0] == 0 else small[4 * m : 4 * m + 1]
        scale_sum = jnp.zeros((1, D), F32) if chunks[0] == 0 else small[4 * m + 1 : 4 * m + 2]
        for c in chunks:
            part = slice(c * chunk, (c + 1) * chunk)
            for side in range(2):
                back_copy(m, side, c).wait_recv()
            grad_normed = (
                grad_near[m, part]
                + back_near[m, 0, part].astype(F32)
                + back_near[m, 1, part].astype(F32)
            )
            unit, inverse = normalize(x_in[m, part])
            scaled = grad_normed * (1.0 + modulation(m, 1))
            grad_in = mixed[m, part] + inverse * (
                scaled - row_mean(scaled) - unit * row_mean(scaled * unit)
            )
            if returning:
                sent_x[m, part] = grad_in.astype(BF16)
                x_copy(m, c).start()
            else:
                mixed[m, part] = grad_in
            shift_sum += column_sum(grad_normed)
            scale_sum += column_sum(grad_normed * unit)
        small[4 * m : 4 * m + 1] = shift_sum
        small[4 * m + 1 : 4 * m + 2] = scale_sum
        if not returning:
            grad_copy(m).start()

    def weight_grad(block):
        if block < 4:
            value = mm_tn(active[:, block * D : (block + 1) * D], grad_low[...])
        elif block < 8:
            value = mm_tn(normed_b[...], slope[:, (block - 4) * D : (block - 3) * D])
        elif block == 8:
            value = mm_tn(attended[...], grad_mixed_low[...])
        elif block == 9:
            value = sum(
                mm_tn(
                    near[m * window + rows : m * window + 2 * rows],
                    grad_query[m * rows : (m + 1) * rows],
                )
                for m in range(MICRO)
            )
        else:
            value = mm_tn(near[...], grad_kv[:, (block - 10) * D : (block - 9) * D])
        grads[block * D : (block + 1) * D] = value.astype(BF16)

    def block_target(block):
        if block < 4:
            return grad_down_out.at[pl.ds(block * D, D)]
        if block < 8:
            return grad_up_out.at[:, pl.ds((block - 4) * D, D)]
        if block == 8:
            return grad_out_out
        return grad_qkv_out.at[:, pl.ds((block - 9) * D, D)]

    task_rows = max(D, 16 * wide)
    tasks = GRAD_ROWS // task_rows
    per_task = task_rows // D

    def order(task):
        if task < 2 and levels > 2:
            return [0] + list(range(2, levels)) + [1]
        return list(range(levels))

    def segment(task, stage):
        base = task * task_rows
        size = task_rows
        for level in order(task)[:stage]:
            size //= 2
            base = base + bit_of(level) * size
        return base, size

    def halving(task, stage):
        level = order(task)[stage]
        base, size = segment(task, stage)
        half = size // 2
        away = pl.multiple_of(base + (1 - bit_of(level)) * half, 16)
        spot = task * task_rows + task_rows - size
        return pltpu.make_async_remote_copy(
            src_ref=grads.at[pl.ds(away, half)],
            dst_ref=landing.at[pl.ds(spot, half)],
            send_sem=ring_send.at[task, stage],
            recv_sem=ring_recv.at[task, stage],
            device_id=(sec, partner(level)),
            device_id_type=MESH,
        )

    def doubling(task, stage):
        level = order(task)[levels - 1 - stage]
        base, size = segment(task, levels - stage)
        place = pl.ds(pl.multiple_of(base, 16), size)
        return pltpu.make_async_remote_copy(
            src_ref=gathered.at[place],
            dst_ref=gathered.at[place],
            send_sem=ring_send.at[task, levels + stage],
            recv_sem=ring_recv.at[task, levels + stage],
            device_id=(sec, partner(level)),
            device_id_type=MESH,
        )

    def reduce_step(task, stage):
        if stage == 0:
            halving(task, 0).start()
            return
        if stage <= levels:
            halving(task, stage - 1).wait_recv()
            base, size = segment(task, stage)
            spot = task * task_rows + task_rows - 2 * size
            place = pl.ds(pl.multiple_of(base, 16), size)
            value = grads[place, :].astype(F32) + landing[spot : spot + size].astype(F32)
            if stage < levels:
                grads[place, :] = value.astype(BF16)
                halving(task, stage).start()
            else:
                gathered[place, :] = value.astype(BF16)
                doubling(task, 0).start()
            return
        doubling(task, stage - levels - 1).wait_recv()
        if stage < 2 * levels:
            doubling(task, stage - levels).start()
        else:
            for block in range(task * per_task, (task + 1) * per_task):
                pltpu.make_async_copy(
                    gathered.at[pl.ds(block * D, D)], block_target(block), store_sem.at[2 + block]
                ).start()

    def small_copy(level):
        return pltpu.make_async_remote_copy(
            src_ref=small.at[pl.ds(0, SMALL_ROWS)] if level == 0 else small_landing.at[1, level],
            dst_ref=small_landing.at[0, level],
            send_sem=small_send.at[level],
            recv_sem=small_recv.at[level],
            device_id=(sec, partner(level)),
            device_id_type=MESH,
        )

    def small_step(level):
        if level > 0:
            small_copy(level - 1).wait_recv()
            held = small[...] if level == 1 else small_landing[1, level - 1]
            value = held + small_landing[0, level - 1]
            if level == levels:
                small_landing[1, 0] = value
                return
            small_landing[1, level] = value
        small_copy(level).start()

    small[13:SMALL_ROWS] = jnp.zeros((SMALL_ROWS - 13, D), F32)

    @pl.when(first)
    def _():
        prepare(0, False)
        prepare(1, False)

    make_modulation((2, 3))
    count_slots()

    @pl.when(second)
    def _():
        prepare(0, True)
        prepare(1, True)

    for m in range(MICRO):
        forward(m)

    @pl.when(first)
    def _():
        for m in range(MICRO):
            for c in range(CHUNKS):
                x_copy(m, c).wait_send()

    take_grad(0)
    backward_gate(0)
    backward_dense(0)
    backward_heads(0, range(HEADS))
    send_back(0)

    @pl.when(first)
    def _():
        near_grad(0)

    take_grad(1)

    @pl.when(second)
    def _():
        backward_gate(1)
        backward_dense(1)
        backward_heads(1, range(3))
        near_grad(0)
        finish(0, True, range(2))
        backward_heads(1, range(3, HEADS))
        finish(0, True, range(2, CHUNKS))
        send_back(1)
        near_grad(1)
        finish(1, True)

    def end(m):
        if m == 1:
            near_grad(1)
        finish(m, False)

    extras = {"gate": functools.partial(backward_gate, 1)}
    extras["dense"] = functools.partial(backward_dense, 1)
    for h in range(HEADS):
        extras[f"head{h}"] = functools.partial(backward_heads, 1, [h])
    extras["back"] = functools.partial(send_back, 1)
    extras["end0"] = functools.partial(end, 0)
    extras["end1"] = functools.partial(end, 1)

    if levels == 4 and tasks == 12:
        plan = ORDER
    else:
        plan = list(extras)
        for moment in range(tasks + 4 * levels):
            for stage in range(2 * levels, -1, -1):
                if 0 <= moment - 2 * stage < tasks:
                    plan.append((moment - 2 * stage, stage))
    ended = False
    level = 0
    for item in plan:
        if item in extras:
            pl.when(first)(extras[item])
            ended = ended or item == "end1"
            continue
        task, stage = item
        if stage == 0:
            for block in range(task * per_task, (task + 1) * per_task):
                weight_grad(block)
        reduce_step(task, stage)
        if ended and level <= levels and stage >= 2:
            small_step(level)
            level += 1
    for level in range(level, levels + 1):
        small_step(level)
    small_out[...] = small_landing[1, 0]

    for m in range(MICRO):
        for side in range(2):
            for c in range(CHUNKS):
                halo_copy(m, side, c).wait_send()
                back_copy(m, side, c).wait_send()

    @pl.when(first)
    def _():
        for m in range(MICRO):
            grad_copy(m).wait()

    @pl.when(second)
    def _():
        for m in range(MICRO):
            for c in range(CHUNKS):
                x_copy(m, c).wait_send()

    for task in range(tasks):
        for stage in range(levels):
            halving(task, stage).wait_send()
            doubling(task, stage).wait_send()
    for level in range(levels):
        small_copy(level).wait_send()
    for block in range(12):
        pltpu.make_async_copy(
            gathered.at[pl.ds(block * D, D)], block_target(block), store_sem.at[2 + block]
        ).wait()


def shards(
    features,
    sigma_embed,
    cotangent,
    neighbours,
    valid_slots,
    ada_weight,
    ada_bias,
    qkv_weight,
    out_weight,
    up_weight,
    up_bias,
    down_weight,
    down_bias,
):
    rows = features.shape[1]
    wide = lax.axis_size("wide")
    sections = lax.axis_size("section")
    levels = wide.bit_length() - 1
    tasks = GRAD_ROWS // max(D, 16 * wide)
    window = 3 * rows
    every = pl.BlockSpec(memory_space=pl.ANY)
    vmem = pl.BlockSpec(memory_space=pltpu.VMEM)
    dma = pltpu.SemaphoreType.DMA
    outs = pl.pallas_call(
        functools.partial(layer_kernel, sections, wide),
        out_shape=(
            jax.ShapeDtypeStruct((1, MICRO, rows, D), F32),
            jax.ShapeDtypeStruct((D, 3 * D), BF16),
            jax.ShapeDtypeStruct((D, D), BF16),
            jax.ShapeDtypeStruct((D, FF), BF16),
            jax.ShapeDtypeStruct((FF, D), BF16),
            jax.ShapeDtypeStruct((SMALL_ROWS, D), F32),
        ),
        in_specs=[every, every, vmem, vmem, vmem, every, vmem, every, every, every, vmem, every, vmem],
        out_specs=[every, every, every, every, every, vmem],
        scratch_shapes=[
            pltpu.VMEM((D, 3 * D), BF16),
            pltpu.VMEM((D, D), BF16),
            pltpu.VMEM((D, FF), BF16),
            pltpu.VMEM((FF, D), BF16),
            pltpu.VMEM((MICRO, 4 * D), F32),
            pltpu.VMEM((rows, NEIGHBOURS), F32),
            pltpu.VMEM((rows, window), F32),
            pltpu.VMEM((MICRO, rows, D), F32),
            pltpu.VMEM((MICRO, rows, D), F32),
            pltpu.VMEM((MICRO * window, D), BF16),
            pltpu.VMEM((MICRO, rows, D), BF16),
            pltpu.VMEM((MICRO * window, 2 * D), BF16),
            pltpu.VMEM((MICRO * rows, D), BF16),
            pltpu.VMEM((MICRO, rows, HEADS), F32),
            pltpu.VMEM((MICRO, rows, D), F32),
            pltpu.VMEM((MICRO * rows, D), BF16),
            pltpu.VMEM((MICRO * rows, FF), BF16),
            pltpu.VMEM((MICRO * rows, FF), BF16),
            pltpu.VMEM((MICRO * rows, D), BF16),
            pltpu.VMEM((MICRO * rows, D), BF16),
            pltpu.VMEM((MICRO * rows, D), BF16),
            pltpu.VMEM((MICRO * window, 2 * D), BF16),
            pltpu.VMEM((rows, D), BF16),
            pltpu.VMEM((MICRO, rows, D), F32),
            pltpu.VMEM((MICRO, 2, rows, D), BF16),
            pltpu.VMEM((MICRO, 2, rows, D), BF16),
            pltpu.VMEM((MICRO, rows, D), BF16),
            pltpu.VMEM((MICRO, rows, D), BF16),
            pltpu.VMEM((GRAD_ROWS, D), BF16),
            pltpu.VMEM((GRAD_ROWS, D), BF16),
            pltpu.VMEM((GRAD_ROWS, D), BF16),
            pltpu.VMEM((SMALL_ROWS, D), F32),
            pltpu.VMEM((2, levels, SMALL_ROWS, D), F32),
            dma((12,)),
            dma((2 + 12,)),
            dma((MICRO, 2, CHUNKS)),
            dma((MICRO, 2, CHUNKS)),
            dma((MICRO, 2, CHUNKS)),
            dma((MICRO, 2, CHUNKS)),
            dma((MICRO, CHUNKS)),
            dma((MICRO, CHUNKS)),
            dma((tasks, 2 * levels)),
            dma((tasks, 2 * levels)),
            dma((levels,)),
            dma((levels,)),
        ],
        compiler_params=pltpu.CompilerParams(
            collective_id=1, has_side_effects=True, vmem_limit_bytes=63 * 1024 * 1024
        ),
        name="layers",
    )(
        features,
        cotangent,
        sigma_embed,
        neighbours.T,
        valid_slots.T,
        ada_weight,
        ada_bias,
        qkv_weight,
        out_weight,
        up_weight,
        up_bias,
        down_weight,
        down_bias,
    )
    boundary, grad_qkv, grad_out, grad_up, grad_down, small = outs
    return pl.pallas_call(
        widen_kernel,
        out_shape=(
            jax.ShapeDtypeStruct(boundary.shape, F32),
            jax.ShapeDtypeStruct((1, D, 4 * D), F32),
            jax.ShapeDtypeStruct((1, 4 * D), F32),
            jax.ShapeDtypeStruct((1, D, 3 * D), F32),
            jax.ShapeDtypeStruct((1, D, D), F32),
            jax.ShapeDtypeStruct((1, D, FF), F32),
            jax.ShapeDtypeStruct((1, FF), F32),
            jax.ShapeDtypeStruct((1, FF, D), F32),
            jax.ShapeDtypeStruct((1, D), F32),
        ),
        in_specs=[every] * 5 + [vmem, vmem],
        out_specs=[every, every, vmem, every, every, every, vmem, every, vmem],
        scratch_shapes=[
            pltpu.VMEM((GRAD_ROWS, D), BF16),
            pltpu.VMEM((GRAD_ROWS, D), F32),
            pltpu.VMEM((4 * D, D), F32),
            pltpu.VMEM(boundary.shape, F32),
            dma((13,)),
            dma((17,)),
        ],
        compiler_params=pltpu.CompilerParams(vmem_limit_bytes=60 * 1024 * 1024),
        name="widen",
    )(boundary, grad_qkv, grad_out, grad_up, grad_down, small, sigma_embed)


def widen_kernel(
    boundary,
    grad_qkv,
    grad_out,
    grad_up,
    grad_down,
    small,
    sigma,
    boundary_wide,
    ada_wide,
    ada_bias_wide,
    qkv_wide,
    out_wide,
    up_wide,
    up_bias_wide,
    down_wide,
    down_bias_wide,
    narrow,
    broad,
    outer,
    held,
    load_sem,
    store_sem,
):
    def blocks(down, up, out, qkv):
        return (
            [down.at[pl.ds(j * D, D)] for j in range(4)]
            + [up.at[:, pl.ds(j * D, D)] for j in range(4)]
            + [out]
            + [qkv.at[:, pl.ds(j * D, D)] for j in range(3)]
        )

    rest = pltpu.make_async_copy(boundary, held, load_sem.at[12])
    rest.start()
    loads, stores = [], []
    for i, source in enumerate(blocks(grad_down, grad_up, grad_out, grad_qkv)):
        loads.append(pltpu.make_async_copy(source, narrow.at[pl.ds(i * D, D)], load_sem.at[i]))
        loads[-1].start()
    column = jnp.transpose(sigma[...].astype(F32))
    for j in range(4):
        part = slice(j * D, (j + 1) * D)
        outer[part] = column[:, 0:1] * small[j : j + 1] + column[:, 1:2] * small[4 + j : 5 + j]
        ada_bias_wide[:, part] = small[j : j + 1] + small[4 + j : 5 + j]
        up_bias_wide[:, part] = small[8 + j : 9 + j]
        stores.append(
            pltpu.make_async_copy(
                outer.at[pl.ds(j * D, D)], ada_wide.at[0, :, pl.ds(j * D, D)], store_sem.at[12 + j]
            )
        )
        stores[-1].start()
    down_bias_wide[...] = small[12:13]
    rest.wait()
    stores.append(pltpu.make_async_copy(held, boundary_wide, store_sem.at[16]))
    stores[-1].start()
    targets = blocks(down_wide.at[0], up_wide.at[0], out_wide.at[0], qkv_wide.at[0])
    for i, target in enumerate(targets):
        loads[i].wait()
        part = slice(i * D, (i + 1) * D)
        broad[part] = narrow[part].astype(F32)
        stores.append(pltpu.make_async_copy(broad.at[pl.ds(i * D, D)], target, store_sem.at[i]))
        stores[-1].start()
    for copy in stores:
        copy.wait()


def solution(mesh):
    return jax.shard_map(
        shards,
        mesh=mesh,
        in_specs=(
            P(None, "wide", None),
            P(),
            P(None, "wide", None),
            P("wide", None),
            P("wide", None),
            P("section", None, None),
            P("section", None),
            P("section", None, None),
            P("section", None, None),
            P("section", None, None),
            P("section", None),
            P("section", None, None),
            P("section", None),
        ),
        out_specs=(
            P("section", None, "wide", None),
            P("section", None, None),
            P("section", None),
            P("section", None, None),
            P("section", None, None),
            P("section", None, None),
            P("section", None),
            P("section", None, None),
            P("section", None),
        ),
        check_vma=False,
    )
```
